128 devices in a mesh: dp: 4 (over y_hi, core), fsdp: 32 (over y_lo, x, z).
Axes of the slice: x: 4, y: 4 (y_hi: 2, y_lo: 2; y = y_hi * 2 + y_lo), z: 4, core: 2. Of those that a mesh axis runs over, the one named last changes fastest.
Arguments:
- activations: bfloat16 [2048, 8192], P('dp', 'fsdp'), may hold values from -6 to 6
- out_grads: bfloat16 [2048, 8192], P('dp', 'fsdp'), may hold values from -6 to 6
- query_acts: bfloat16 [128, 8192], P(None, 'fsdp'), may hold values from -6 to 6
- query_grads: bfloat16 [128, 8192], P(None, 'fsdp'), may hold values from -6 to 6
- eig_in: bfloat16 [8192, 8192], P('fsdp'), may hold values from -0.125 to 0.125
- eig_out: bfloat16 [8192, 8192], P('fsdp'), may hold values from -0.0625 to 0.0625
- example_ids: int32 [4, 512], P('dp'), may hold values from 0 to 7, never falling along the last dimension, each value on 1 to 128 neighbouring positions
Outputs:
- corrections: float32 [8192, 8192], P('fsdp')
- scores: float32 [32, 32], P(None, 'dp')
The draws below stay inside these ranges and needn't reach their ends.
Inputs may be any that keep to these rules, and one draw needn't show every extreme that they name: `example_ids`: in each group's row the ids never fall, every QA pair 0 to 7 has 1 to 128 tokens, and one has exactly 128.
All inputs are finite; a program needn't handle non-finite values.
Results may differ from the reference program's by a relative error of at most 0.0055.
Values may be sent and summed in bfloat16 or wider, within the bound.
A program may use at most 192 MiB of HBM per device.

```python
import math
import jax
import jax.numpy as jnp
import numpy as np
from jax import lax

D_IN = 8192
D_OUT = 8192
TOK_GRP = 512
MOST = 128
EX = 8
NQ = 32
QTOK = 4
QROWS = 128
TOKENS = 2048
EXAMPLES = 32
N_DP = 4


def raised(drawn, rng, source, target, parts, factor):
    owner, partner = [(jnp.arange(drawn.shape[dim]) // (drawn.shape[dim] // parts)).reshape([-1 if axis == dim else 1 for axis in range(drawn.ndim)]) for dim in (source, target)]
    chosen = jax.random.permutation(rng, parts)[partner]
    strong = (owner == chosen) | (owner == (partner + parts // 2) % parts)
    return jnp.where(strong, factor * drawn, drawn)


def block_levels(key, extent, shards, smallest, top_value):
    loudness = 1.0
    for dim, parts in shards:
        steps = jax.random.uniform(jax.random.fold_in(jax.random.fold_in(key, 6), dim), (parts,), jnp.float32, smallest / len(shards), top_value / len(shards))
        loudness = loudness * jnp.repeat(jnp.exp(steps), extent[dim] // parts).reshape((-1,) + (1,) * (len(extent) - 1 - dim))
    return loudness


def profile(count, total, limit, slope):
    weights = [(1 << 20) // math.isqrt(rank ** slope) + 1 for rank in range(2, count + 1)]
    spare, holding = total - limit - (count - 1), [1] * (count - 1)
    while spare > 0:
        candidates = [i for i in range(count - 1) if holding[i] < limit]
        pool, budget = sum([weights[i] for i in candidates]), spare
        for i in candidates:
            extra = min(limit - holding[i], max(1, budget * weights[i] // pool), spare)
            holding[i] = holding[i] + extra
            spare = spare - extra
    return np.array([limit] + holding)


def uneven(own_key, number_of, total, reach, slope):
    if number_of == 2:
        one = jax.random.randint(own_key, (), max(1, total - reach), min(reach, total - 1) + 1)
        return jnp.stack([one, total - one])
    lengths = jnp.asarray(profile(number_of, total, reach, slope), jnp.int32)
    couples = (number_of - 1) // 2
    source_of, sink = lengths[1:1 + 2 * couples:2], lengths[2:2 + 2 * couples:2]
    room = jnp.minimum(source_of - 1, reach - sink)
    moved = jax.random.randint(jax.random.fold_in(own_key, 1), (couples,), 0, 1 << 20) % (room + 1)
    lengths = lengths.at[1:1 + 2 * couples:2].set(source_of - moved).at[2:2 + 2 * couples:2].set(sink + moved)
    return lengths[jax.random.permutation(jax.random.fold_in(own_key, 2), number_of)]


def bell_draw(stream_key, extent, spread, limit, cuts=(), kind=jnp.bfloat16):
    array = jax.random.normal(stream_key, extent, jnp.float32) * spread
    if len(cuts) > 0:
        array = block_levels(stream_key, extent, cuts, -0.22, 0.18) * array
    return jnp.clip(array, min=-limit, max=limit).astype(kind)


def bell_draw_with(own_key, extent, spread, most, pieces, heavy, kind=jnp.bfloat16):
    array = spread * jax.random.normal(own_key, extent, jnp.float32)
    if pieces:
        array = array * block_levels(own_key, extent, pieces, -0.22, 0.18)
    return jnp.clip(raised(array, jax.random.fold_in(own_key, 3), *heavy), -most, most).astype(kind)


def setup_inputs(seed: int = 0) -> dict:
    seeds = jax.random.split(jax.random.key(seed), 8)
    activations = bell_draw(seeds[0], (TOKENS, D_IN), 1.0, 6.0, ((0, 4), (1, 32)))
    out_grads = bell_draw(seeds[1], (TOKENS, D_OUT), 1.0, 6.0, ((0, 4), (1, 32)))
    query_acts = bell_draw(seeds[2], (QROWS, D_IN), 1.0, 6.0, ((1, 32),))
    query_grads = bell_draw(seeds[3], (QROWS, D_OUT), 1.0, 6.0, ((1, 32),))
    eig_in = bell_draw_with(seeds[4], (D_IN, D_IN), D_IN ** -0.5, 0.125, ((0, 32),), (0, 1, 32, 2.75))
    eig_out = bell_draw(seeds[5], (D_OUT, D_OUT), D_OUT ** -0.5, 0.0625, ((0, 32),))
    example_ids = jax.vmap(lambda own: jnp.searchsorted(jnp.cumsum(uneven(own, EX, TOK_GRP, MOST, 0)), jnp.arange(TOK_GRP), side="right"))(jax.random.split(seeds[6], N_DP)).reshape((N_DP, TOK_GRP)).astype(jnp.int32)
    return dict(activations=activations, out_grads=out_grads, query_acts=query_acts, query_grads=query_grads, eig_in=eig_in, eig_out=eig_out, example_ids=example_ids)


def example_block(rot_in, rot_out, example_ids, position):
    group = position // EX
    example = position % EX
    ids_row = lax.dynamic_index_in_dim(example_ids, group, 0, keepdims=False)
    first_local = jnp.sum((ids_row < example).astype(jnp.int32))
    first_local = jnp.minimum(first_local, TOK_GRP - MOST).astype(jnp.int32)
    first_row = (group * TOK_GRP + first_local).astype(jnp.int32)
    in_rows = lax.dynamic_slice_in_dim(rot_in, first_row, MOST, 0)
    out_rows = lax.dynamic_slice_in_dim(rot_out, first_row, MOST, 0)
    live_rows = lax.dynamic_slice_in_dim(ids_row, first_local, MOST, 0) == example
    out_rows = jnp.where(live_rows[:, None], out_rows, jnp.zeros_like(out_rows))
    return jnp.dot(in_rows.T, out_rows, preferred_element_type=jnp.float32).astype(jnp.bfloat16)

def reference(activations, out_grads, query_acts, query_grads, eig_in, eig_out, example_ids):
    rot_in = jnp.dot(activations, eig_in, preferred_element_type=jnp.float32).astype(jnp.bfloat16)
    query_in = jnp.dot(query_acts, eig_in, preferred_element_type=jnp.float32).astype(jnp.bfloat16)
    rot_out = jnp.dot(out_grads, eig_out.T, preferred_element_type=jnp.float32).astype(jnp.bfloat16)
    query_out = jnp.dot(query_grads, eig_out.T, preferred_element_type=jnp.float32).astype(jnp.bfloat16)
    positions = jnp.arange(EXAMPLES, dtype=jnp.int32)

    def accumulate(carry_sum, position):
        rotated = example_block(rot_in, rot_out, example_ids, position).astype(jnp.float32)
        return (carry_sum + rotated * rotated, None)
    squares, _ = lax.scan(accumulate, jnp.zeros((D_IN, D_OUT), jnp.float32), positions)
    corrections = squares / EXAMPLES
    damping = 0.5 * jnp.mean(corrections)
    norm_factor = 1.0 / jnp.sqrt(jnp.float32(D_IN) * jnp.float32(D_OUT))

    def score_one(position):
        rotated = example_block(rot_in, rot_out, example_ids, position)
        precond = (rotated.astype(jnp.float32) / (corrections + damping)).astype(jnp.bfloat16)
        partial_value = jnp.dot(precond, query_out.T, preferred_element_type=jnp.float32)
        weighted = partial_value * query_in.T.astype(jnp.float32)
        return lax.optimization_barrier(jnp.sum(weighted.reshape(D_IN, NQ, QTOK), axis=(0, 2))) * norm_factor
    scores = lax.map(score_one, positions).T
    return (corrections, scores)
```

```python
import jax
import jax.numpy as jnp
from jax import lax
from jax.experimental import pallas as pl
from jax.experimental.pallas import tpu as pltpu
from jax.sharding import PartitionSpec as P

D_IN = 8192
D_OUT = 8192
EX = 8
NQ = 32
QTOK = 4
ROWS = 1152
MESH = pl.DeviceIdType.MESH
F32 = jnp.float32
BF16 = jnp.bfloat16


def place():
    dp, fs = lax.axis_index("dp"), lax.axis_index("fsdp")
    return dp // 2, lax.rem(dp, 2), fs // 16, lax.rem(fs // 4, 4), lax.rem(fs, 4)


def device(h, c, y, x, z):
    return (2 * h + c, 16 * y + 4 * x + z)


def greet(partners):
    barrier = pltpu.get_barrier_semaphore()
    for partner in partners:
        pl.semaphore_signal(barrier, 1, device_id=partner, device_id_type=MESH)
    pl.semaphore_wait(barrier, len(partners))


def remote(src, dst, sems, slot, target):
    return pltpu.make_async_remote_copy(
        src_ref=src, dst_ref=dst, send_sem=sems[0].at[slot], recv_sem=sems[1].at[slot],
        device_id=target, device_id_type=MESH,
    )


def rotate_kernel(
    act, grd, qa, qg, eig_in, eig_out, x_out, y_out,
    a_buf, g_buf, u_buf, v_buf,
    xs_buf, xr_buf, vs_buf, vr_buf, xys_buf, xyr_buf, vys_buf, vyr_buf, x_own, v_own,
    loc, h_s, h_r, ag_s, ag_r, gg_s, gg_r, u_s, u_r, v_s, v_r, us_s, us_r, vsib_s, vsib_r,
    x_s, x_r, z_s, z_r, y_s, y_r,
):
    h, c, y, x, z = place()
    oh, oc, oy = 1 - h, 1 - c, 1 - y
    xs = [lax.rem(x + d, 4) for d in range(4)]
    zs = [lax.rem(z + d, 4) for d in range(4)]
    sibling = device(h, oc, y, x, z)
    greet(
        [sibling, device(oh, c, y, x, z), device(h, c, oy, x, z)]
        + [device(h, c, y, xs[d], z) for d in (1, 2, 3)]
        + [device(h, c, y, x, zs[d]) for d in (1, 2, 3)]
        + [device(h, c, oy, x, zs[d]) for d in (1, 2, 3)]
    )
    started = []

    def go(copy):
        copy.start()
        started.append(copy)
        return copy

    ah = go(remote(act, a_buf.at[z, pl.ds(640, 512)], (h_s, h_r), 0, device(oh, c, y, x, z)))
    gh = go(remote(grd, g_buf.at[x, pl.ds(640, 512)], (h_s, h_r), 1, device(oh, c, y, x, z)))
    local = [
        pltpu.make_async_copy(act, a_buf.at[z, pl.ds(0, 512)], loc.at[0]),
        pltpu.make_async_copy(qa, a_buf.at[z, pl.ds(512, 128)], loc.at[1]),
        pltpu.make_async_copy(grd, g_buf.at[x, pl.ds(0, 512)], loc.at[2]),
        pltpu.make_async_copy(qg, g_buf.at[x, pl.ds(512, 128)], loc.at[3]),
    ]
    for copy in local:
        copy.start()
    own = []
    for p in range(4):
        own.append(pltpu.make_async_copy(
            eig_in.at[:, pl.ds(256 * (16 * h + 4 * p + z), 256)], u_buf.at[z, p], loc.at[4 + p]))
        own.append(pltpu.make_async_copy(
            eig_out.at[pl.ds(128 * h, 128), pl.ds(256 * (16 * y + 4 * p + z), 256)],
            v_buf.at[z, p, pl.ds(128 * y, 128)], loc.at[8 + p]))
    for copy in own:
        copy.start()
    for copy in local:
        copy.wait()
    a1, g1 = [], []
    for d in (1, 3, 2):
        mine = pl.ds(0, 640)
        a1.append(go(remote(a_buf.at[z, mine], a_buf.at[z, mine], (ag_s, ag_r), d, device(h, c, y, x, zs[d]))))
        g1.append(go(remote(g_buf.at[x, mine], g_buf.at[x, mine], (gg_s, gg_r), d, device(h, c, y, xs[d], z))))
    u1, v1 = [], []
    for d in (1, 3, 2):
        for p in range(2):
            piece = 2 * c + p
            u1.append(go(remote(
                eig_in.at[:, pl.ds(256 * (16 * h + 4 * piece + zs[d]), 256)], u_buf.at[z, piece],
                (u_s, u_r), 2 * d + p, device(h, c, y, x, zs[d]))))
    for dy, yd in ((0, y), (1, oy)):
        for d in (1, 3, 2, 0):
            if dy == 0 and d == 0:
                continue
            for p in range(2):
                piece = 2 * c + p
                v1.append((dy, d, p, go(remote(
                    eig_out.at[pl.ds(128 * h, 128), pl.ds(256 * (16 * yd + 4 * piece + zs[d]), 256)],
                    v_buf.at[z, piece, pl.ds(128 * y, 128)],
                    (v_s, v_r), 8 * dy + 2 * d + p, device(h, c, yd, x, zs[d])))))
    ah.wait_recv()
    gh.wait_recv()
    other = pl.ds(640, 512)
    for d in (1, 3, 2):
        a1.append(go(remote(a_buf.at[z, other], a_buf.at[z, other], (ag_s, ag_r), 4 + d, device(h, c, y, x, zs[d]))))
        g1.append(go(remote(g_buf.at[x, other], g_buf.at[x, other], (gg_s, gg_r), 4 + d, device(h, c, y, xs[d], z))))
    handed = []
    for n, d in enumerate((1, 3, 2)):
        src = lax.rem(z + 4 - d, 4)
        for p in range(2):
            u1[2 * n + p].wait_recv()
        part = u_buf.at[src, pl.ds(2 * c, 2)]
        handed.append(go(remote(part, part, (us_s, us_r), d, sibling)))
    for copy in own:
        copy.wait()
    for copy in a1:
        copy.wait_recv()
    for copy in handed:
        copy.wait_recv()
    tile = 384
    xsend = []

    def product_in(piece, store):
        def body(i, _):
            rows = pl.ds(pl.multiple_of(i * tile, tile), tile)
            total = jnp.zeros((tile, 256), F32)
            for s in range(4):
                total += jnp.dot(a_buf[s, rows, :], u_buf[s, piece], preferred_element_type=F32)
            store(rows, total)
            return 0
        lax.fori_loop(0, ROWS // tile, body, 0)

    for n, d in enumerate((1, 3, 2, 0)):
        if d:
            def store(rows, total):
                xs_buf[n, rows, :] = total.astype(BF16)
            product_in(xs[d], store)
            xsend.append(go(remote(xs_buf.at[n], xr_buf.at[n], (x_s, x_r), n, device(h, c, y, xs[d], z))))
        else:
            def store(rows, total):
                x_own[rows, :] = total
            product_in(xs[0], store)
    vhanded = []
    arrived = {}
    for dy, d, p, copy in v1:
        copy.wait_recv()
        arrived[(dy, d)] = arrived.get((dy, d), 0) + 1
        if arrived[(dy, d)] == 2:
            src = lax.rem(z + 4 - d, 4)
            part = v_buf.at[src, pl.ds(2 * c, 2), pl.ds(128 * (y if dy == 0 else oy), 128)]
            vhanded.append(go(remote(part, part, (vsib_s, vsib_r), 4 * dy + d, sibling)))
    for copy in g1:
        copy.wait_recv()
    for copy in vhanded:
        copy.wait_recv()
    zsend = []

    def product_out(piece, store):
        def body(i, _):
            rows = pl.ds(pl.multiple_of(i * tile, tile), tile)
            total = jnp.zeros((tile, 256), F32)
            for s in range(4):
                total += lax.dot_general(
                    g_buf[s, rows, :], v_buf[piece, s], (((1,), (1,)), ((), ())), preferred_element_type=F32)
            store(rows, total)
            return 0
        lax.fori_loop(0, ROWS // tile, body, 0)

    for n, d in enumerate((1, 3, 2, 0)):
        if d:
            def store(rows, total):
                vs_buf[n, rows, :] = total.astype(BF16)
            product_out(zs[d], store)
            zsend.append(go(remote(vs_buf.at[n], vr_buf.at[n], (z_s, z_r), n, device(h, c, y, x, zs[d]))))
        else:
            def store(rows, total):
                v_own[rows, :] = total
            product_out(zs[0], store)

    def add_up(own_ref, got, send):
        def body(i, _):
            rows = pl.ds(pl.multiple_of(i * 128, 128), 128)
            total = own_ref[rows, :]
            for n in range(3):
                total += got[n, rows, :].astype(F32)
            own_ref[rows, :] = total
            send[rows, :] = jnp.where(y == 0, total[:, 128:], total[:, :128]).astype(BF16)
            return 0
        lax.fori_loop(0, ROWS // 128, body, 0)

    partner = device(h, c, oy, x, z)
    for copy in xsend:
        copy.wait_recv()
    add_up(x_own, xr_buf, xys_buf)
    xy = go(remote(xys_buf, xyr_buf, (y_s, y_r), 0, partner))
    for copy in zsend:
        copy.wait_recv()
    add_up(v_own, vr_buf, vys_buf)
    vy = go(remote(vys_buf, vyr_buf, (y_s, y_r), 1, partner))

    def block_at(n):
        return jnp.where(n < 4, 4 * h + n, jnp.where(n == 4, 8, 4 * oh + n - 5))

    def finish(own_ref, got, out, turn):
        def body(i, _):
            rows = pl.ds(pl.multiple_of(i * 128, 128), 128)
            total = own_ref[rows, :]
            mine = jnp.where(y == 0, total[:, :128], total[:, 128:]) + got[rows, :].astype(F32)
            out[block_at(i)] = (mine.T if turn else mine).astype(BF16)
            return 0
        lax.fori_loop(0, 9, body, 0)

    xy.wait_recv()
    finish(x_own, xyr_buf, x_out, True)
    vy.wait_recv()
    finish(v_own, vyr_buf, y_out, False)
    for copy in started:
        copy.wait_send()


def rotate(act, grd, qa, qg, eig_in, eig_out):
    dma = pltpu.SemaphoreType.DMA
    any_ = pl.BlockSpec(memory_space=pl.ANY)
    vmem = pl.BlockSpec(memory_space=pltpu.VMEM)
    return pl.pallas_call(
        rotate_kernel,
        out_shape=(jax.ShapeDtypeStruct((9, 128, 128), BF16), jax.ShapeDtypeStruct((9, 128, 128), BF16)),
        in_specs=[any_] * 6,
        out_specs=(vmem, vmem),
        scratch_shapes=[
            pltpu.VMEM((4, ROWS, 256), BF16),
            pltpu.VMEM((4, ROWS, 256), BF16),
            pltpu.VMEM((4, 4, 256, 256), BF16),
            pltpu.VMEM((4, 4, 256, 256), BF16),
            pltpu.VMEM((3, ROWS, 256), BF16),
            pltpu.VMEM((3, ROWS, 256), BF16),
            pltpu.VMEM((3, ROWS, 256), BF16),
            pltpu.VMEM((3, ROWS, 256), BF16),
            pltpu.VMEM((ROWS, 128), BF16),
            pltpu.VMEM((ROWS, 128), BF16),
            pltpu.VMEM((ROWS, 128), BF16),
            pltpu.VMEM((ROWS, 128), BF16),
            pltpu.VMEM((ROWS, 256), F32),
            pltpu.VMEM((ROWS, 256), F32),
            dma((12,)),
            dma((2,)), dma((2,)),
            dma((8,)), dma((8,)),
            dma((8,)), dma((8,)),
            dma((8,)), dma((8,)),
            dma((16,)), dma((16,)),
            dma((4,)), dma((4,)),
            dma((8,)), dma((8,)),
            dma((3,)), dma((3,)),
            dma((3,)), dma((3,)),
            dma((2,)), dma((2,)),
        ],
        compiler_params=pltpu.CompilerParams(
            collective_id=1, has_side_effects=True, vmem_limit_bytes=40 * 2**20),
        cost_estimate=pl.CostEstimate(flops=5 * 10**9, bytes_accessed=10**7, transcendentals=0),
        name="rotate",
    )(act, grd, qa, qg, eig_in, eig_out)


def score_kernel(
    x_mine, y_mine, ids, corr, scores,
    x_all, y_all, id_all, rot, sq, sq_got, c_stage, acc, red, red_got, red2, red2_got, blks,
    loc, gx_s, gx_r, gy_s, gy_r, id_s, id_r, sq_s, sq_r, t_s, t_r, o_s, o_r, f_s, f_r, p_s, p_r,
):
    h, c, y, x, z = place()
    oh, oc, oy = 1 - h, 1 - c, 1 - y
    yy = 2 * h + y
    xs = [lax.rem(x + d, 4) for d in range(4)]
    zs = [lax.rem(z + d, 4) for d in range(4)]
    ys = [lax.rem(yy + d, 4) for d in range(4)]
    sibling = device(h, oc, y, x, z)

    def at_y(v):
        return device(v // 2, c, lax.rem(v, 2), x, z)

    plane = []
    for dy in range(4):
        for dx in range(4):
            if dy or dx:
                plane.append(device(ys[dy] // 2, c, lax.rem(ys[dy], 2), xs[dx], z))
    greet([sibling] + plane + [device(h, c, y, x, zs[d]) for d in (1, 2, 3)])
    started = []

    def go(copy):
        copy.start()
        started.append(copy)
        return copy

    def x_slot(xv, yv):
        return x_all.at[:, pl.ds(pl.multiple_of(128 * (2 * xv + yv), 128), 128), :]

    def y_slot(zv, hv):
        return y_all.at[:, :, pl.ds(pl.multiple_of(128 * (2 * zv + hv), 128), 128)]

    across_h, across_y = device(oh, c, y, x, z), device(h, c, oy, x, z)
    ids_copy = go(remote(ids, id_all.at[h], (id_s, id_r), 0, across_h))
    xy = go(remote(x_mine, x_slot(x, y), (gx_s, gx_r), 0, across_y))
    yh = go(remote(y_mine, y_slot(z, h), (gy_s, gy_r), 0, across_h))
    got = []
    for d in (1, 3, 2):
        got.append(go(remote(x_mine, x_slot(x, y), (gx_s, gx_r), d, device(h, c, y, xs[d], z))))
        got.append(go(remote(y_mine, y_slot(z, h), (gy_s, gy_r), d, device(h, c, y, x, zs[d]))))
    local = [
        pltpu.make_async_copy(x_mine, x_slot(x, y), loc.at[0]),
        pltpu.make_async_copy(y_mine, y_slot(z, h), loc.at[1]),
        pltpu.make_async_copy(ids, id_all.at[h], loc.at[2]),
    ]
    for copy in local:
        copy.start()
    xy.wait_recv()
    for d in (1, 3, 2):
        got.append(go(remote(x_slot(x, oy), x_slot(x, oy), (gx_s, gx_r), 4 + d, device(h, c, y, xs[d], z))))
    yh.wait_recv()
    for d in (1, 3, 2):
        got.append(go(remote(y_slot(z, oh), y_slot(z, oh), (gy_s, gy_r), 4 + d, device(h, c, y, x, zs[d]))))
    for copy in local:
        copy.wait()
    ids_copy.wait_recv()
    for g in range(2):
        row = id_all[g]
        for e in range(EX):
            first = jnp.sum((row < e).astype(jnp.int32))
            blks[8 * g + e] = jnp.minimum(first // 128, 2)
    for copy in got:
        copy.wait_recv()

    def quarter(kt, _):
        rows = pl.ds(pl.multiple_of(256 * kt, 256), 256)

        def pair(n, _):
            g, e = n // 8, lax.rem(n, 8)
            blk = blks[n]
            parts = []
            for b in range(2):
                keep = id_all[g, blk + b] == e
                parts.append(jnp.where(keep, x_all[4 * g + blk + b, rows, :].astype(F32), 0.0).astype(BF16))
            left = jnp.concatenate(parts, axis=1)
            for it in range(2):
                cols = pl.ds(512 * it, 512)
                right = jnp.concatenate(
                    [y_all[4 * g + blk, :, cols], y_all[4 * g + blk + 1, :, cols]], axis=0)
                value = jnp.dot(left, right, preferred_element_type=F32).astype(BF16)
                rot[n, rows, cols] = value
                wide = value.astype(F32)

                @pl.when(n == 0)
                def _():
                    sq[kt, :, cols] = wide * wide

                @pl.when(n > 0)
                def _():
                    sq[kt, :, cols] += wide * wide
            return 0

        lax.fori_loop(0, 2 * EX, pair, 0)
        copy = remote(sq.at[kt], sq_got.at[kt], (sq_s, sq_r), kt, sibling)
        copy.start()
        return 0

    lax.fori_loop(0, 4, quarter, 0)

    def add_up(kt, total):
        copy = remote(sq.at[kt], sq_got.at[kt], (sq_s, sq_r), kt, sibling)
        copy.wait()

        def chunk(i, total):
            part = pl.ds(pl.multiple_of(32 * i, 32), 32)
            value = (sq[kt, part, :] + sq_got[kt, part, :]) * (1.0 / 32.0)
            sq[kt, part, :] = value
            for a in range(4):
                for b in range(8):
                    total = total + value[8 * a:8 * a + 8, 128 * b:128 * b + 128]
            return total

        total = lax.fori_loop(0, 8, chunk, total)
        c_stage[kt] = sq[kt, pl.ds(pl.multiple_of(128 * c, 128), 128), :].astype(BF16)
        return total

    total = lax.fori_loop(0, 4, add_up, jnp.zeros((8, 128), F32))

    def spread(value, n, buf, got_buf, sems, where):
        buf[n] = value
        copies = [go(remote(buf.at[n], got_buf.at[n, d - 1], sems, 3 * n + d - 1, where(d))) for d in (1, 2, 3)]
        for copy in copies:
            copy.wait_recv()
        return buf[n] + got_buf[n, 0] + got_buf[n, 1] + got_buf[n, 2]

    steps = (
        lambda d: device(h, c, y, x, zs[d]),
        lambda d: device(h, c, y, xs[d], z),
        lambda d: at_y(ys[d]),
    )
    for n in range(3):
        total = spread(total, n, red, red_got, (t_s, t_r), steps[n])
    damping = 0.5 * (jnp.sum(total) / (float(D_IN) * float(D_OUT)))

    def slab(yv, xv):
        return corr.at[pl.ds(pl.multiple_of(128 * c, 128), 128),
                       pl.ds(pl.multiple_of(1024 * (4 * yv + xv), 1024), 1024)]

    me = 4 * y + x

    def is_me(hv, xv):
        return jnp.logical_and(jnp.logical_and(hv == h, h == y), xv == x)

    def hand_out(start):
        for hd in range(2):
            for d in range(4):
                hv, xv = (h, oh)[hd], xs[d]
                slot = 4 * hd + d
                copy = pltpu.make_async_remote_copy(
                    src_ref=c_stage.at[xv], dst_ref=slab(y, x), send_sem=o_s.at[slot], recv_sem=o_r.at[me],
                    device_id=device(hv, c, h, xv, z), device_id_type=MESH)
                run = copy.start if start else copy.wait_send
                if hd == 0 and d == 0:
                    @pl.when(h != y)
                    def _():
                        run()

                    @pl.when(h == y)
                    def _():
                        own = pltpu.make_async_copy(c_stage.at[x], slab(y, x), loc.at[3])
                        if start:
                            own.start()
                        else:
                            own.wait()
                else:
                    run()

    hand_out(True)

    def second(kt, _):
        rows = pl.ds(pl.multiple_of(256 * kt, 256), 256)

        def invert(i, _):
            part = pl.ds(pl.multiple_of(32 * i, 32), 32)
            sq[kt, part, :] = 1.0 / (sq[kt, part, :] + damping)
            return 0

        lax.fori_loop(0, 8, invert, 0)
        query_in = x_all[8, rows, :].astype(F32)

        def pair(n, _):
            cond = (rot[n, rows, :].astype(F32) * sq[kt]).astype(BF16)
            part = lax.dot_general(
                cond, y_all[8], (((1,), (1,)), ((), ())), preferred_element_type=F32)
            weighted = part * query_in
            value = jnp.sum(weighted, axis=0, keepdims=True)

            @pl.when(kt == 0)
            def _():
                acc[pl.ds(n, 1), :] = value

            @pl.when(kt > 0)
            def _():
                acc[pl.ds(n, 1), :] += value
            return 0

        lax.fori_loop(0, 2 * EX, pair, 0)
        return 0

    lax.fori_loop(0, 4, second, 0)
    hand_out(False)

    def forward(i, _):
        yv, xv = i // 4, lax.rem(i, 4)
        mine = jnp.logical_and(h == y, i == me)

        @pl.when(jnp.logical_not(mine))
        def _():
            pltpu.make_async_remote_copy(
                src_ref=c_stage.at[0], dst_ref=slab(yv, xv), send_sem=o_s.at[0], recv_sem=o_r.at[i],
                device_id=sibling, device_id_type=MESH).wait_recv()
        pltpu.make_async_remote_copy(
            src_ref=slab(yv, xv), dst_ref=slab(yv, xv), send_sem=f_s.at[i], recv_sem=f_r.at[i],
            device_id=sibling, device_id_type=MESH).start()
        return 0

    lax.fori_loop(0, 8, forward, 0)
    value = acc[...]
    for n in range(3):
        value = spread(value, n, red2, red2_got, (p_s, p_r), steps[n])
    scores[...] = value

    def last(i, _):
        yv, xv = i // 4, lax.rem(i, 4)
        pltpu.make_async_remote_copy(
            src_ref=slab(yv, xv), dst_ref=slab(yv, xv), send_sem=f_s.at[i], recv_sem=f_r.at[i],
            device_id=sibling, device_id_type=MESH).wait()
        return 0

    lax.fori_loop(0, 8, last, 0)
    for copy in started:
        copy.wait_send()


def score(x_mine, y_mine, ids):
    dma = pltpu.SemaphoreType.DMA
    vmem = pl.BlockSpec(memory_space=pltpu.VMEM)
    return pl.pallas_call(
        score_kernel,
        out_shape=(jax.ShapeDtypeStruct((256, D_OUT), BF16), jax.ShapeDtypeStruct((2 * EX, 128), F32)),
        in_specs=[vmem] * 3,
        out_specs=(pl.BlockSpec(memory_space=pltpu.VMEM), vmem),
        scratch_shapes=[
            pltpu.VMEM((9, 1024, 128), BF16),
            pltpu.VMEM((9, 128, 1024), BF16),
            pltpu.VMEM((2, 4, 1, 128), jnp.int32),
            pltpu.VMEM((2 * EX, 1024, 1024), BF16),
            pltpu.VMEM((4, 256, 1024), F32),
            pltpu.VMEM((4, 256, 1024), F32),
            pltpu.VMEM((4, 128, 1024), BF16),
            pltpu.VMEM((2 * EX, 128), F32),
            pltpu.VMEM((3, 8, 128), F32),
            pltpu.VMEM((3, 3, 8, 128), F32),
            pltpu.VMEM((3, 2 * EX, 128), F32),
            pltpu.VMEM((3, 3, 2 * EX, 128), F32),
            pltpu.SMEM((2 * EX,), jnp.int32),
            dma((4,)),
            dma((8,)), dma((8,)),
            dma((8,)), dma((8,)),
            dma((1,)), dma((1,)),
            dma((4,)), dma((4,)),
            dma((9,)), dma((9,)),
            dma((8,)), dma((8,)),
            dma((8,)), dma((8,)),
            dma((9,)), dma((9,)),
        ],
        compiler_params=pltpu.CompilerParams(
            collective_id=2, has_side_effects=True, vmem_limit_bytes=60 * 2**20),
        cost_estimate=pl.CostEstimate(flops=2 * 10**10, bytes_accessed=10**7, transcendentals=0),
        name="score",
    )(x_mine, y_mine, ids)


def per_device(activations, out_grads, query_acts, query_grads, eig_in, eig_out, example_ids):
    x_mine, y_mine = rotate(activations, out_grads, query_acts, query_grads, eig_in, eig_out)
    corr, sums = score(x_mine, y_mine, example_ids.reshape(4, 1, 128))
    h = lax.axis_index("dp") // 2
    mine = lax.dynamic_slice_in_dim(sums, EX * h, EX, 0)
    norm_factor = 1.0 / jnp.sqrt(jnp.float32(D_IN) * jnp.float32(D_OUT))
    scores = jnp.sum(mine.reshape(EX, NQ, QTOK), axis=2).T * norm_factor
    return corr.astype(F32), scores


def solution(mesh):
    return jax.shard_map(
        per_device,
        mesh=mesh,
        in_specs=(
            P("dp", "fsdp"),
            P("dp", "fsdp"),
            P(None, "fsdp"),
            P(None, "fsdp"),
            P("fsdp", None),
            P("fsdp", None),
            P("dp", None),
        ),
        out_specs=(P("fsdp", None), P(None, "dp")),
        check_vma=False,
    )
```

```python
import jax
import jax.numpy as jnp
from jax import lax
from jax.experimental import pallas as pl
from jax.experimental.pallas import tpu as pltpu
from jax.sharding import PartitionSpec as P

D_IN = 8192
D_OUT = 8192
EX = 8
NQ = 32
QTOK = 4
ROWS = 1152
MESH = pl.DeviceIdType.MESH
F32 = jnp.float32
BF16 = jnp.bfloat16


def place():
    dp, fs = lax.axis_index("dp"), lax.axis_index("fsdp")
    return dp // 2, lax.rem(dp, 2), fs // 16, lax.rem(fs // 4, 4), lax.rem(fs, 4)


def device(h, c, y, x, z):
    return (2 * h + c, 16 * y + 4 * x + z)


def greet(partners):
    barrier = pltpu.get_barrier_semaphore()
    for partner in partners:
        pl.semaphore_signal(barrier, 1, device_id=partner, device_id_type=MESH)
    pl.semaphore_wait(barrier, len(partners))


def remote(src, dst, sems, slot, target):
    return pltpu.make_async_remote_copy(
        src_ref=src, dst_ref=dst, send_sem=sems[0].at[slot], recv_sem=sems[1].at[slot],
        device_id=target, device_id_type=MESH,
    )


def rotate_kernel(
    act, grd, qa, qg, eig_in, eig_out, x_out, y_out,
    a_buf, g_buf, u_buf, v_buf,
    xs_buf, xr_buf, vs_buf, vr_buf, xys_buf, xyr_buf, vys_buf, vyr_buf, x_own, v_own,
    loc, h_s, h_r, ag_s, ag_r, gg_s, gg_r, u_s, u_r, v_s, v_r, us_s, us_r, vsib_s, vsib_r,
    x_s, x_r, z_s, z_r, y_s, y_r,
):
    h, c, y, x, z = place()
    oh, oc, oy = 1 - h, 1 - c, 1 - y
    xs = [lax.rem(x + d, 4) for d in range(4)]
    zs = [lax.rem(z + d, 4) for d in range(4)]
    sibling = device(h, oc, y, x, z)
    greet(
        [sibling, device(oh, c, y, x, z), device(h, c, oy, x, z)]
        + [device(h, c, y, xs[d], z) for d in (1, 2, 3)]
        + [device(h, c, y, x, zs[d]) for d in (1, 2, 3)]
        + [device(h, c, oy, x, zs[d]) for d in (1, 2, 3)]
    )
    started = []

    def go(copy):
        copy.start()
        started.append(copy)
        return copy

    ah = go(remote(act, a_buf.at[z, pl.ds(640, 512)], (h_s, h_r), 0, device(oh, c, y, x, z)))
    gh = go(remote(grd, g_buf.at[x, pl.ds(640, 512)], (h_s, h_r), 1, device(oh, c, y, x, z)))
    local = [
        pltpu.make_async_copy(act, a_buf.at[z, pl.ds(0, 512)], loc.at[0]),
        pltpu.make_async_copy(qa, a_buf.at[z, pl.ds(512, 128)], loc.at[1]),
        pltpu.make_async_copy(grd, g_buf.at[x, pl.ds(0, 512)], loc.at[2]),
        pltpu.make_async_copy(qg, g_buf.at[x, pl.ds(512, 128)], loc.at[3]),
    ]
    for copy in local:
        copy.start()
    own = []
    for p in range(4):
        for q in range(2):
            own.append(pltpu.make_async_copy(
                eig_in.at[:, pl.ds(256 * (16 * q + 4 * p + z) + 128 * h, 128)],
                u_buf.at[z, p, :, pl.ds(128 * q, 128)], loc.at[12 + 2 * p + q]))
        own.append(pltpu.make_async_copy(
            eig_out.at[pl.ds(128 * h, 128), pl.ds(256 * (16 * y + 4 * p + z), 256)],
            v_buf.at[z, p, pl.ds(128 * y, 128)], loc.at[8 + p]))
    for copy in own:
        copy.start()
    for copy in local:
        copy.wait()
    a1, g1 = [], []
    for d in (1, 3, 2):
        mine = pl.ds(0, 640)
        a1.append(go(remote(a_buf.at[z, mine], a_buf.at[z, mine], (ag_s, ag_r), d, device(h, c, y, x, zs[d]))))
        g1.append(go(remote(g_buf.at[x, mine], g_buf.at[x, mine], (gg_s, gg_r), d, device(h, c, y, xs[d], z))))
    u1, v1 = [], []
    for d in (1, 3, 2):
        for p in range(4):
            u1.append(go(remote(
                eig_in.at[:, pl.ds(256 * (16 * c + 4 * p + zs[d]) + 128 * h, 128)],
                u_buf.at[z, p, :, pl.ds(128 * c, 128)],
                (u_s, u_r), 4 * d + p, device(h, c, y, x, zs[d]))))
    for dy, yd in ((0, y), (1, oy)):
        for d in (1, 3, 2, 0):
            if dy == 0 and d == 0:
                continue
            for p in range(2):
                piece = 2 * c + p
                v1.append((dy, d, p, go(remote(
                    eig_out.at[pl.ds(128 * h, 128), pl.ds(256 * (16 * yd + 4 * piece + zs[d]), 256)],
                    v_buf.at[z, piece, pl.ds(128 * y, 128)],
                    (v_s, v_r), 8 * dy + 2 * d + p, device(h, c, yd, x, zs[d])))))
    ah.wait_recv()
    gh.wait_recv()
    other = pl.ds(640, 512)
    for d in (1, 3, 2):
        a1.append(go(remote(a_buf.at[z, other], a_buf.at[z, other], (ag_s, ag_r), 4 + d, device(h, c, y, x, zs[d]))))
        g1.append(go(remote(g_buf.at[x, other], g_buf.at[x, other], (gg_s, gg_r), 4 + d, device(h, c, y, xs[d], z))))
    handed = []
    for n, d in enumerate((1, 3, 2)):
        src = lax.rem(z + 4 - d, 4)
        for p in range(4):
            u1[4 * n + p].wait_recv()
        part = u_buf.at[src, :, :, pl.ds(128 * c, 128)]
        handed.append(go(remote(part, part, (us_s, us_r), d, sibling)))
    for copy in own:
        copy.wait()
    for copy in a1:
        copy.wait_recv()
    for copy in handed:
        copy.wait_recv()
    tile = 384
    xsend = []

    def product_in(piece, store):
        def body(i, _):
            rows = pl.ds(pl.multiple_of(i * tile, tile), tile)
            total = jnp.zeros((tile, 256), F32)
            for s in range(4):
                total += jnp.dot(a_buf[s, rows, :], u_buf[s, piece], preferred_element_type=F32)
            store(rows, total)
            return 0
        lax.fori_loop(0, ROWS // tile, body, 0)

    for n, d in enumerate((1, 3, 2, 0)):
        if d:
            def store(rows, total):
                xs_buf[n, rows, :] = total.astype(BF16)
            product_in(xs[d], store)
            xsend.append(go(remote(xs_buf.at[n], xr_buf.at[n], (x_s, x_r), n, device(h, c, y, xs[d], z))))
        else:
            def store(rows, total):
                x_own[rows, :] = total
            product_in(xs[0], store)
    vhanded = []
    arrived = {}
    for dy, d, p, copy in v1:
        copy.wait_recv()
        arrived[(dy, d)] = arrived.get((dy, d), 0) + 1
        if arrived[(dy, d)] == 2:
            src = lax.rem(z + 4 - d, 4)
            part = v_buf.at[src, pl.ds(2 * c, 2), pl.ds(128 * (y if dy == 0 else oy), 128)]
            vhanded.append(go(remote(part, part, (vsib_s, vsib_r), 4 * dy + d, sibling)))
    for copy in g1:
        copy.wait_recv()
    for copy in vhanded:
        copy.wait_recv()
    zsend = []

    def product_out(piece, store):
        def body(i, _):
            rows = pl.ds(pl.multiple_of(i * tile, tile), tile)
            total = jnp.zeros((tile, 256), F32)
            for s in range(4):
                total += lax.dot_general(
                    g_buf[s, rows, :], v_buf[piece, s], (((1,), (1,)), ((), ())), preferred_element_type=F32)
            store(rows, total)
            return 0
        lax.fori_loop(0, ROWS // tile, body, 0)

    for n, d in enumerate((1, 3, 2, 0)):
        if d:
            def store(rows, total):
                vs_buf[n, rows, :] = total.astype(BF16)
            product_out(zs[d], store)
            zsend.append(go(remote(vs_buf.at[n], vr_buf.at[n], (z_s, z_r), n, device(h, c, y, x, zs[d]))))
        else:
            def store(rows, total):
                v_own[rows, :] = total
            product_out(zs[0], store)

    def add_up(own_ref, got, send):
        def body(i, _):
            rows = pl.ds(pl.multiple_of(i * 128, 128), 128)
            total = own_ref[rows, :]
            for n in range(3):
                total += got[n, rows, :].astype(F32)
            own_ref[rows, :] = total
            send[rows, :] = jnp.where(y == 0, total[:, 128:], total[:, :128]).astype(BF16)
            return 0
        lax.fori_loop(0, ROWS // 128, body, 0)

    partner = device(h, c, oy, x, z)
    for copy in xsend:
        copy.wait_recv()
    add_up(x_own, xr_buf, xys_buf)
    xy = go(remote(xys_buf, xyr_buf, (y_s, y_r), 0, partner))
    for copy in zsend:
        copy.wait_recv()
    add_up(v_own, vr_buf, vys_buf)
    vy = go(remote(vys_buf, vyr_buf, (y_s, y_r), 1, partner))

    def block_at(n):
        return jnp.where(n < 4, 4 * h + n, jnp.where(n == 4, 8, 4 * oh + n - 5))

    def finish(own_ref, got, out, turn):
        def body(i, _):
            rows = pl.ds(pl.multiple_of(i * 128, 128), 128)
            total = own_ref[rows, :]
            mine = jnp.where(y == 0, total[:, :128], total[:, 128:]) + got[rows, :].astype(F32)
            out[block_at(i)] = (mine.T if turn else mine).astype(BF16)
            return 0
        lax.fori_loop(0, 9, body, 0)

    xy.wait_recv()
    finish(x_own, xyr_buf, x_out, True)
    vy.wait_recv()
    finish(v_own, vyr_buf, y_out, False)
    for copy in started:
        copy.wait_send()


def rotate(act, grd, qa, qg, eig_in, eig_out):
    dma = pltpu.SemaphoreType.DMA
    any_ = pl.BlockSpec(memory_space=pl.ANY)
    vmem = pl.BlockSpec(memory_space=pltpu.VMEM)
    return pl.pallas_call(
        rotate_kernel,
        out_shape=(jax.ShapeDtypeStruct((9, 128, 128), BF16), jax.ShapeDtypeStruct((9, 128, 128), BF16)),
        in_specs=[any_] * 6,
        out_specs=(vmem, vmem),
        scratch_shapes=[
            pltpu.VMEM((4, ROWS, 256), BF16),
            pltpu.VMEM((4, ROWS, 256), BF16),
            pltpu.VMEM((4, 4, 256, 256), BF16),
            pltpu.VMEM((4, 4, 256, 256), BF16),
            pltpu.VMEM((3, ROWS, 256), BF16),
            pltpu.VMEM((3, ROWS, 256), BF16),
            pltpu.VMEM((3, ROWS, 256), BF16),
            pltpu.VMEM((3, ROWS, 256), BF16),
            pltpu.VMEM((ROWS, 128), BF16),
            pltpu.VMEM((ROWS, 128), BF16),
            pltpu.VMEM((ROWS, 128), BF16),
            pltpu.VMEM((ROWS, 128), BF16),
            pltpu.VMEM((ROWS, 256), F32),
            pltpu.VMEM((ROWS, 256), F32),
            dma((20,)),
            dma((2,)), dma((2,)),
            dma((8,)), dma((8,)),
            dma((8,)), dma((8,)),
            dma((16,)), dma((16,)),
            dma((16,)), dma((16,)),
            dma((4,)), dma((4,)),
            dma((8,)), dma((8,)),
            dma((3,)), dma((3,)),
            dma((3,)), dma((3,)),
            dma((2,)), dma((2,)),
        ],
        compiler_params=pltpu.CompilerParams(
            collective_id=1, has_side_effects=True, vmem_limit_bytes=60 * 2**20),
        cost_estimate=pl.CostEstimate(flops=5 * 10**9, bytes_accessed=10**7, transcendentals=0),
        name="rotate",
    )(act, grd, qa, qg, eig_in, eig_out)


def score_kernel(
    x_mine, y_mine, ids, corr, scores,
    x_all, y_all, id_all, rot, sq, sq_got, c_stage, acc, red, red_got, red2, red2_got, blks,
    loc, gx_s, gx_r, gy_s, gy_r, id_s, id_r, sq_s, sq_r, t_s, t_r, o_s, o_r, f_s, f_r, p_s, p_r,
):
    h, c, y, x, z = place()
    oh, oc, oy = 1 - h, 1 - c, 1 - y
    yy = 2 * h + y
    xs = [lax.rem(x + d, 4) for d in range(4)]
    xb = [lax.rem(x + 4 - d, 4) for d in range(4)]
    zs = [lax.rem(z + d, 4) for d in range(4)]
    ys = [lax.rem(yy + d, 4) for d in range(4)]
    sibling = device(h, oc, y, x, z)
    greet(
        [sibling, device(h, c, oy, x, z), device(oh, c, oy, x, z)]
        + [device(h, c, y, xs[d], z) for d in (1, 2, 3)]
        + [device(oh, c, y, xs[d], z) for d in (0, 1, 2, 3)]
        + [device(h, c, y, x, zs[d]) for d in (1, 2, 3)]
    )
    started = []

    def go(copy):
        copy.start()
        started.append(copy)
        return copy

    def x_slot(xv, hv):
        return x_all.at[:, pl.ds(pl.multiple_of(128 * (2 * xv + hv), 128), 128), :]

    def y_slot(zv, yv):
        return y_all.at[:, :, pl.ds(pl.multiple_of(128 * (2 * zv + yv), 128), 128)]

    across_h, across_y = device(oh, c, y, x, z), device(h, c, oy, x, z)
    ids_copy = go(remote(ids, id_all.at[h], (id_s, id_r), 0, across_h))
    xh = go(remote(x_mine, x_slot(x, h), (gx_s, gx_r), 0, across_h))
    yy_copy = go(remote(y_mine, y_slot(z, y), (gy_s, gy_r), 0, across_y))
    got = []
    for d in (1, 3, 2):
        got.append(go(remote(x_mine, x_slot(x, h), (gx_s, gx_r), d, device(h, c, y, xs[d], z))))
        got.append(go(remote(y_mine, y_slot(z, y), (gy_s, gy_r), d, device(h, c, y, x, zs[d]))))
    local = [
        pltpu.make_async_copy(x_mine, x_slot(x, h), loc.at[0]),
        pltpu.make_async_copy(y_mine, y_slot(z, y), loc.at[1]),
        pltpu.make_async_copy(ids, id_all.at[h], loc.at[2]),
    ]
    for copy in local:
        copy.start()
    xh.wait_recv()
    for d in (1, 3, 2):
        got.append(go(remote(x_slot(x, oh), x_slot(x, oh), (gx_s, gx_r), 4 + d, device(h, c, y, xs[d], z))))
    yy_copy.wait_recv()
    for d in (1, 3, 2):
        got.append(go(remote(y_slot(z, oy), y_slot(z, oy), (gy_s, gy_r), 4 + d, device(h, c, y, x, zs[d]))))
    for copy in local:
        copy.wait()
    ids_copy.wait_recv()
    for g in range(2):
        row = id_all[g]
        for e in range(EX):
            first = jnp.sum((row < e).astype(jnp.int32))
            blks[8 * g + e] = jnp.minimum(first // 128, 2)
    sq[...] = jnp.zeros_like(sq)
    acc[...] = jnp.zeros_like(acc)
    for copy in got:
        copy.wait_recv()

    def quarter(kt):
        rows = pl.ds(pl.multiple_of(256 * kt, 256), 256)

        def pairs(m, _):
            lefts, blocks = [], []
            for u in range(4):
                n = 4 * m + u
                g, e = n // 8, lax.rem(n, 8)
                blk = blks[n]
                parts = []
                for b in range(2):
                    keep = id_all[g, blk + b] == e
                    parts.append(jnp.where(keep, x_all[4 * g + blk + b, rows, :].astype(F32), 0.0).astype(BF16))
                lefts.append(jnp.concatenate(parts, axis=1))
                blocks.append(4 * g + blk)
            for it in range(4):
                cols = pl.ds(256 * it, 256)
                total = sq[kt, :, cols]
                for u in range(4):
                    right = jnp.concatenate([y_all[blocks[u], :, cols], y_all[blocks[u] + 1, :, cols]], axis=0)
                    value = jnp.dot(lefts[u], right, preferred_element_type=F32).astype(BF16)
                    rot[4 * m + u, rows, cols] = value
                    wide = value.astype(F32)
                    total = total + wide * wide
                sq[kt, :, cols] = total
            return 0

        lax.fori_loop(0, EX // 2, pairs, 0)

    def sq_copy(kt):
        return remote(sq.at[kt], sq_got.at[kt], (sq_s, sq_r), kt, sibling)

    def add_up(kt, total):
        sq_copy(kt).wait()

        def chunk(i, total):
            part = pl.ds(pl.multiple_of(32 * i, 32), 32)
            value = (sq[kt, part, :] + sq_got[kt, part, :]) * (1.0 / 32.0)
            sq[kt, part, :] = value
            for a in range(4):
                for b in range(8):
                    total = total + value[8 * a:8 * a + 8, 128 * b:128 * b + 128]
            return total

        total = lax.fori_loop(0, 8, chunk, total)
        c_stage[kt] = sq[kt, pl.ds(pl.multiple_of(128 * c, 128), 128), :].astype(BF16)
        return total

    def slab(xv, hv):
        return corr.at[2 * xv + hv, pl.ds(pl.multiple_of(128 * c, 128), 128), :]

    def out_copies(j):
        copies = []
        for hd in range(2):
            if hd or j:
                copies.append(pltpu.make_async_remote_copy(
                    src_ref=c_stage.at[xs[j]], dst_ref=slab(x, h), send_sem=o_s.at[4 * hd + j],
                    recv_sem=o_r.at[4 * hd + j], device_id=device((h, oh)[hd], c, y, xs[j], z),
                    device_id_type=MESH))
        return copies

    own_out = pltpu.make_async_copy(c_stage.at[x], slab(x, h), loc.at[3])
    total = jnp.zeros((8, 128), F32)
    for j in range(4):
        quarter(xs[j])
        sq_copy(xs[j]).start()
        if j:
            total = add_up(xs[j - 1], total)
            for copy in out_copies(j - 1):
                copy.start()
            if j == 1:
                own_out.start()
    total = add_up(xs[3], total)

    def spread(value, n, buf, got_buf, sems, where):
        buf[n] = value
        copies = [go(remote(buf.at[n], got_buf.at[n, d - 1], sems, 3 * n + d - 1, where(d))) for d in (1, 2, 3)]
        for copy in copies:
            copy.wait_recv()
        return buf[n] + got_buf[n, 0] + got_buf[n, 1] + got_buf[n, 2]

    def at_y(v):
        return device(v // 2, c, lax.rem(v, 2), x, z)

    steps = (
        lambda d: device(h, c, y, x, zs[d]),
        lambda d: device(h, c, y, xs[d], z),
        lambda d: at_y(ys[d]),
    )
    for n in range(3):
        total = spread(total, n, red, red_got, (t_s, t_r), steps[n])
    damping = 0.5 * (jnp.sum(total) / (float(D_IN) * float(D_OUT)))
    for copy in out_copies(3):
        copy.start()

    def second(kt):
        rows = pl.ds(pl.multiple_of(256 * kt, 256), 256)

        def invert(i, _):
            part = pl.ds(pl.multiple_of(32 * i, 32), 32)
            sq[kt, part, :] = 1.0 / (sq[kt, part, :] + damping)
            return 0

        lax.fori_loop(0, 8, invert, 0)

        def pairs(m, _):
            query_in = x_all[8, rows, :].astype(F32)
            sums = [None] * 4
            for it in range(4):
                cols = pl.ds(256 * it, 256)
                factor = sq[kt, :, cols]
                query_out = y_all[8, :, cols]
                for u in range(4):
                    cond = (rot[4 * m + u, rows, cols].astype(F32) * factor).astype(BF16)
                    part = lax.dot_general(
                        cond, query_out, (((1,), (1,)), ((), ())), preferred_element_type=F32)
                    sums[u] = part if it == 0 else sums[u] + part
            for u in range(4):
                acc[pl.ds(4 * m + u, 1), :] += jnp.sum(sums[u] * query_in, axis=0, keepdims=True)
            return 0

        lax.fori_loop(0, EX // 2, pairs, 0)

    def hand_on(xv, hv):
        return remote(slab(xv, hv), slab(xv, hv), (f_s, f_r), 2 * xv + hv, sibling)

    for j in range(4):
        second(xs[j])
        for copy in out_copies(j):
            copy.wait()
        if j == 0:
            own_out.wait()
        for hv in (h, oh):
            hand_on(xb[j], hv).start()
    value = acc[...]
    for n in range(3):
        value = spread(value, n, red2, red2_got, (p_s, p_r), steps[n])
    scores[...] = value
    for j in range(4):
        for hv in (h, oh):
            hand_on(xb[j], hv).wait()
    for copy in started:
        copy.wait_send()


def score(x_mine, y_mine, ids):
    dma = pltpu.SemaphoreType.DMA
    vmem = pl.BlockSpec(memory_space=pltpu.VMEM)
    return pl.pallas_call(
        score_kernel,
        out_shape=(jax.ShapeDtypeStruct((8, 256, 1024), BF16), jax.ShapeDtypeStruct((2 * EX, 128), F32)),
        in_specs=[vmem] * 3,
        out_specs=(pl.BlockSpec(memory_space=pltpu.VMEM), vmem),
        scratch_shapes=[
            pltpu.VMEM((9, 1024, 128), BF16),
            pltpu.VMEM((9, 128, 1024), BF16),
            pltpu.VMEM((2, 4, 1, 128), jnp.int32),
            pltpu.VMEM((2 * EX, 1024, 1024), BF16),
            pltpu.VMEM((4, 256, 1024), F32),
            pltpu.VMEM((4, 256, 1024), F32),
            pltpu.VMEM((4, 128, 1024), BF16),
            pltpu.VMEM((2 * EX, 128), F32),
            pltpu.VMEM((3, 8, 128), F32),
            pltpu.VMEM((3, 3, 8, 128), F32),
            pltpu.VMEM((3, 2 * EX, 128), F32),
            pltpu.VMEM((3, 3, 2 * EX, 128), F32),
            pltpu.SMEM((2 * EX,), jnp.int32),
            dma((4,)),
            dma((8,)), dma((8,)),
            dma((8,)), dma((8,)),
            dma((1,)), dma((1,)),
            dma((4,)), dma((4,)),
            dma((9,)), dma((9,)),
            dma((8,)), dma((8,)),
            dma((8,)), dma((8,)),
            dma((9,)), dma((9,)),
        ],
        compiler_params=pltpu.CompilerParams(
            collective_id=2, has_side_effects=True, vmem_limit_bytes=60 * 2**20),
        cost_estimate=pl.CostEstimate(flops=2 * 10**10, bytes_accessed=10**7, transcendentals=0),
        name="score",
    )(x_mine, y_mine, ids)


def widen_kernel(corr, out, stage, sems):
    def copy(n):
        yv, xv = n // 4, n % 4
        return pltpu.make_async_copy(stage.at[n % 2], out.at[:, pl.ds(1024 * (4 * yv + xv), 1024)], sems.at[n % 2])

    for n in range(8):
        yv, xv = n // 4, n % 4
        if n >= 2:
            copy(n - 2).wait()
        for zv in range(4):
            for hv in range(2):
                stage[n % 2, :, pl.ds(128 * (2 * zv + hv), 128)] = corr[
                    2 * xv + hv, :, pl.ds(128 * (2 * zv + yv), 128)].astype(F32)
        copy(n).start()
    copy(6).wait()
    copy(7).wait()


def widen(corr):
    return pl.pallas_call(
        widen_kernel,
        out_shape=jax.ShapeDtypeStruct((256, D_OUT), F32),
        in_specs=[pl.BlockSpec(memory_space=pltpu.VMEM)],
        out_specs=pl.BlockSpec(memory_space=pl.ANY),
        scratch_shapes=[pltpu.VMEM((2, 256, 1024), F32), pltpu.SemaphoreType.DMA((2,))],
        compiler_params=pltpu.CompilerParams(vmem_limit_bytes=60 * 2**20),
        name="widen",
    )(corr)


def per_device(activations, out_grads, query_acts, query_grads, eig_in, eig_out, example_ids):
    x_mine, y_mine = rotate(activations, out_grads, query_acts, query_grads, eig_in, eig_out)
    corr, sums = score(x_mine, y_mine, example_ids.reshape(4, 1, 128))
    h = lax.axis_index("dp") // 2
    mine = lax.dynamic_slice_in_dim(sums, EX * h, EX, 0)
    norm_factor = 1.0 / jnp.sqrt(jnp.float32(D_IN) * jnp.float32(D_OUT))
    scores = jnp.sum(mine.reshape(EX, NQ, QTOK), axis=2).T * norm_factor
    return widen(corr), scores


def solution(mesh):
    return jax.shard_map(
        per_device,
        mesh=mesh,
        in_specs=(
            P("dp", "fsdp"),
            P("dp", "fsdp"),
            P(None, "fsdp"),
            P(None, "fsdp"),
            P("fsdp", None),
            P("fsdp", None),
            P("dp", None),
        ),
        out_specs=(P("fsdp", None), P(None, "dp")),
        check_vma=False,
    )
```

```python
import jax
import jax.numpy as jnp
from jax import lax
from jax.experimental import pallas as pl
from jax.experimental.pallas import tpu as pltpu
from jax.sharding import PartitionSpec as P

D_IN = 8192
D_OUT = 8192
EX = 8
NQ = 32
QTOK = 4
ROWS = 1152
MESH = pl.DeviceIdType.MESH
F32 = jnp.float32
BF16 = jnp.bfloat16


def place():
    dp, fs = lax.axis_index("dp"), lax.axis_index("fsdp")
    return dp // 2, lax.rem(dp, 2), fs // 16, lax.rem(fs // 4, 4), lax.rem(fs, 4)


def device(h, c, y, x, z):
    return (2 * h + c, 16 * y + 4 * x + z)


def greet(partners):
    barrier = pltpu.get_barrier_semaphore()
    for partner in partners:
        pl.semaphore_signal(barrier, 1, device_id=partner, device_id_type=MESH)
    pl.semaphore_wait(barrier, len(partners))


def remote(src, dst, sems, slot, target):
    return pltpu.make_async_remote_copy(
        src_ref=src, dst_ref=dst, send_sem=sems[0].at[slot], recv_sem=sems[1].at[slot],
        device_id=target, device_id_type=MESH,
    )


def rotate_kernel(
    act, grd, qa, qg, eig_in, eig_out, x_out, y_out,
    a_buf, g_buf, u_buf, v_buf, in_bufs, out_bufs,
    loc, h_s, h_r, ag_s, ag_r, gg_s, gg_r, u_s, u_r, v_s, v_r, us_s, us_r, vsib_s, vsib_r,
    in_sems, out_sems,
):
    h, c, y, x, z = place()
    oh, oc, oy = 1 - h, 1 - c, 1 - y
    xs = [lax.rem(x + d, 4) for d in range(4)]
    zs = [lax.rem(z + d, 4) for d in range(4)]
    sibling = device(h, oc, y, x, z)
    partner = device(h, c, oy, x, z)
    greet(
        [sibling, device(oh, c, y, x, z), partner]
        + [device(h, c, y, xs[d], z) for d in (1, 2, 3)]
        + [device(h, c, y, x, zs[d]) for d in (1, 2, 3)]
        + [device(h, c, oy, x, zs[d]) for d in (1, 2, 3)]
    )
    started = []

    def go(copy):
        copy.start()
        started.append(copy)
        return copy

    ah = go(remote(act, a_buf.at[z, pl.ds(640, 512)], (h_s, h_r), 0, device(oh, c, y, x, z)))
    gh = go(remote(grd, g_buf.at[x, pl.ds(640, 512)], (h_s, h_r), 1, device(oh, c, y, x, z)))
    local = [
        pltpu.make_async_copy(act, a_buf.at[z, pl.ds(0, 512)], loc.at[0]),
        pltpu.make_async_copy(qa, a_buf.at[z, pl.ds(512, 128)], loc.at[1]),
        pltpu.make_async_copy(grd, g_buf.at[x, pl.ds(0, 512)], loc.at[2]),
        pltpu.make_async_copy(qg, g_buf.at[x, pl.ds(512, 128)], loc.at[3]),
    ]
    for copy in local:
        copy.start()
    u1 = []
    for d in (1, 3, 2):
        for p in range(4):
            u1.append(go(remote(
                eig_in.at[:, pl.ds(256 * (16 * c + 4 * p + zs[d]) + 128 * h, 128)],
                u_buf.at[z, p, :, pl.ds(128 * c, 128)],
                (u_s, u_r), 4 * d + p, device(h, c, y, x, zs[d]))))
    for copy in local:
        copy.wait()
    mine, other = pl.ds(0, 640), pl.ds(640, 512)
    a1, g1, a2, g2 = [], [], [], []
    for d in (1, 3, 2):
        a1.append(go(remote(a_buf.at[z, mine], a_buf.at[z, mine], (ag_s, ag_r), d, device(h, c, y, x, zs[d]))))
        g1.append(go(remote(g_buf.at[x, mine], g_buf.at[x, mine], (gg_s, gg_r), d, device(h, c, y, xs[d], z))))
    own = []
    for p in range(4):
        for q in range(2):
            own.append(pltpu.make_async_copy(
                eig_in.at[:, pl.ds(256 * (16 * q + 4 * p + z) + 128 * h, 128)],
                u_buf.at[z, p, :, pl.ds(128 * q, 128)], loc.at[12 + 2 * p + q]))
        own.append(pltpu.make_async_copy(
            eig_out.at[pl.ds(128 * h, 128), pl.ds(256 * (16 * y + 4 * p + z), 256)],
            v_buf.at[z, p, pl.ds(128 * y, 128)], loc.at[8 + p]))
    for copy in own:
        copy.start()
    ah.wait_recv()
    gh.wait_recv()
    for d in (1, 3, 2):
        a2.append(go(remote(a_buf.at[z, other], a_buf.at[z, other], (ag_s, ag_r), 4 + d, device(h, c, y, x, zs[d]))))
        g2.append(go(remote(g_buf.at[x, other], g_buf.at[x, other], (gg_s, gg_r), 4 + d, device(h, c, y, xs[d], z))))
    handed = []
    for n, d in enumerate((1, 3, 2)):
        src = lax.rem(z + 4 - d, 4)
        for p in range(4):
            u1[4 * n + p].wait_recv()
        part = u_buf.at[src, :, :, pl.ds(128 * c, 128)]
        handed.append(go(remote(part, part, (us_s, us_r), d, sibling)))
    for copy in own:
        copy.wait()
    for copy in a1:
        copy.wait_recv()
    v1 = []
    for dy, yd in ((1, oy), (0, y)):
        for d in (1, 3, 2, 0):
            if dy == 0 and d == 0:
                continue
            for p in range(2):
                piece = 2 * c + p
                v1.append((dy, d, p, go(remote(
                    eig_out.at[pl.ds(128 * h, 128), pl.ds(256 * (16 * yd + 4 * piece + zs[d]), 256)],
                    v_buf.at[z, piece, pl.ds(128 * y, 128)],
                    (v_s, v_r), 8 * dy + 2 * d + p, device(h, c, yd, x, zs[d])))))
    for copy in handed:
        copy.wait_recv()

    def halves(total):
        low, high = total[:, :128], total[:, 128:]
        return jnp.where(y == 0, low, high), jnp.where(y == 0, high, low)

    def rows_loop(first, count, tile, body):
        def step(i, _):
            start = pl.multiple_of(i * tile, tile)
            body(pl.ds(start, tile), pl.ds(pl.multiple_of(first + start, 64), tile))
            return 0
        lax.fori_loop(0, count // tile, step, 0)

    def side(product, bufs, sems, ring, coords):
        r_send, r_got, r_own, q_send, q_got, p_send, p_got, p_own, w_send, w_got, w_own = bufs
        r_s, r_r, w_s, w_r, y_s, y_r = sems
        sent = {}

        def ring_first():
            sent["ring"] = []
            for n, d in enumerate((1, 3, 2, 0)):
                if d:
                    def body(rows, src):
                        r_send[n, rows, :] = product(src, coords[d], 320).astype(BF16)
                    rows_loop(0, 640, 320, body)
                    sent["ring"].append(go(remote(r_send.at[n], r_got.at[n], (r_s, r_r), n, ring(d))))
                else:
                    def body(rows, src):
                        r_own[rows, :] = product(src, coords[0], 320)
                    rows_loop(0, 640, 320, body)

        def partner_first():
            for d in range(4):
                def body(rows, src):
                    keep, give = halves(product(src, coords[d], 256))
                    p_own[d, rows, :] = keep
                    p_send[coords[d], rows, :] = give.astype(BF16)
                rows_loop(640, 512, 256, body)
            sent["partner"] = go(remote(p_send, p_got, (y_s, y_r), 0, partner))

        def partner_then_ring():
            sent["partner"].wait_recv()
            sent["late"] = []
            for n, d in enumerate((1, 3, 2, 0)):
                def body(rows, _):
                    total = p_own[d, rows, :] + p_got[coords[d], rows, :].astype(F32)
                    if d:
                        w_send[n, rows, :] = total.astype(BF16)
                    else:
                        w_own[rows, :] = total
                rows_loop(0, 512, 256, body)
                if d:
                    sent["late"].append(go(remote(w_send.at[n], w_got.at[n], (w_s, w_r), n, ring(d))))

        def ring_then_partner():
            for copy in sent["ring"]:
                copy.wait_recv()

            def body(rows, _):
                total = r_own[rows, :]
                for n in range(3):
                    total += r_got[n, rows, :].astype(F32)
                r_own[rows, :] = total
                q_send[rows, :] = halves(total)[1].astype(BF16)
            rows_loop(0, 640, 128, body)
            sent["last"] = go(remote(q_send, q_got, (y_s, y_r), 1, partner))

        def finish(out, turn):
            for copy in sent["late"]:
                copy.wait_recv()

            def late(i, _):
                rows = pl.ds(pl.multiple_of(i * 128, 128), 128)
                total = w_own[rows, :]
                for n in range(3):
                    total += w_got[n, rows, :].astype(F32)
                out[4 * oh + i] = (total.T if turn else total).astype(BF16)
                return 0
            lax.fori_loop(0, 4, late, 0)
            sent["last"].wait_recv()

            def first(i, _):
                rows = pl.ds(pl.multiple_of(i * 128, 128), 128)
                total = halves(r_own[rows, :])[0] + q_got[rows, :].astype(F32)
                out[jnp.where(i < 4, 4 * h + i, 8)] = (total.T if turn else total).astype(BF16)
                return 0
            lax.fori_loop(0, 5, first, 0)

        return ring_first, partner_first, partner_then_ring, ring_then_partner, finish

    def product_in(rows, piece, tile):
        total = jnp.zeros((tile, 256), F32)
        for s in range(4):
            total += jnp.dot(a_buf[s, rows, :], u_buf[s, piece], preferred_element_type=F32)
        return total

    def product_out(rows, piece, tile):
        total = jnp.zeros((tile, 256), F32)
        for s in range(4):
            total += lax.dot_general(
                g_buf[s, rows, :], v_buf[piece, s], (((1,), (1,)), ((), ())), preferred_element_type=F32)
        return total

    in_side = side(product_in, in_bufs, in_sems, lambda d: device(h, c, y, xs[d], z), xs)
    out_side = side(product_out, out_bufs, out_sems, lambda d: device(h, c, y, x, zs[d]), zs)
    in_side[0]()
    for copy in a2:
        copy.wait_recv()
    in_side[1]()
    vhanded = []
    for n in range(len(v1) // 2):
        dy, d, _, copy = v1[2 * n]
        copy.wait_recv()
        v1[2 * n + 1][3].wait_recv()
        src = lax.rem(z + 4 - d, 4)
        part = v_buf.at[src, pl.ds(2 * c, 2), pl.ds(128 * (oy if dy else y), 128)]
        vhanded.append(go(remote(part, part, (vsib_s, vsib_r), 4 * dy + d, sibling)))
    for copy in g1 + g2 + vhanded:
        copy.wait_recv()
    out_side[1]()
    out_side[0]()
    in_side[2]()
    in_side[3]()
    out_side[2]()
    out_side[3]()
    in_side[4](x_out, True)
    out_side[4](y_out, False)
    for copy in started:
        copy.wait_send()


def rotate(act, grd, qa, qg, eig_in, eig_out):
    dma = pltpu.SemaphoreType.DMA
    any_ = pl.BlockSpec(memory_space=pl.ANY)
    vmem = pl.BlockSpec(memory_space=pltpu.VMEM)

    def side_bufs():
        return (
            pltpu.VMEM((3, 640, 256), BF16), pltpu.VMEM((3, 640, 256), BF16), pltpu.VMEM((640, 256), F32),
            pltpu.VMEM((640, 128), BF16), pltpu.VMEM((640, 128), BF16),
            pltpu.VMEM((4, 512, 128), BF16), pltpu.VMEM((4, 512, 128), BF16), pltpu.VMEM((4, 512, 128), F32),
            pltpu.VMEM((3, 512, 128), BF16), pltpu.VMEM((3, 512, 128), BF16), pltpu.VMEM((512, 128), F32),
        )

    def side_sems():
        return tuple([dma((3,))] * 4 + [dma((2,))] * 2)

    return pl.pallas_call(
        rotate_kernel,
        out_shape=(jax.ShapeDtypeStruct((9, 128, 128), BF16), jax.ShapeDtypeStruct((9, 128, 128), BF16)),
        in_specs=[any_] * 6,
        out_specs=(vmem, vmem),
        scratch_shapes=[
            pltpu.VMEM((4, ROWS, 256), BF16),
            pltpu.VMEM((4, ROWS, 256), BF16),
            pltpu.VMEM((4, 4, 256, 256), BF16),
            pltpu.VMEM((4, 4, 256, 256), BF16),
            side_bufs(), side_bufs(),
            dma((20,)),
            dma((2,)), dma((2,)),
            dma((8,)), dma((8,)),
            dma((8,)), dma((8,)),
            dma((16,)), dma((16,)),
            dma((16,)), dma((16,)),
            dma((4,)), dma((4,)),
            dma((8,)), dma((8,)),
            side_sems(), side_sems(),
        ],
        compiler_params=pltpu.CompilerParams(
            collective_id=1, has_side_effects=True, vmem_limit_bytes=60 * 2**20),
        cost_estimate=pl.CostEstimate(flops=5 * 10**9, bytes_accessed=10**7, transcendentals=0),
        name="rotate",
    )(act, grd, qa, qg, eig_in, eig_out)


def score_kernel(
    x_mine, y_mine, ids, corr, scores,
    x_all, y_all, id_all, rot, sq, sq_got, c_stage, acc, gram, red, red_got, red2, red2_got, blks,
    loc, gx_s, gx_r, gy_s, gy_r, id_s, id_r, sq_s, sq_r, t_s, t_r, o_s, o_r, f_s, f_r, p_s, p_r,
):
    h, c, y, x, z = place()
    oh, oc, oy = 1 - h, 1 - c, 1 - y
    yy = 2 * h + y
    xs = [lax.rem(x + d, 4) for d in range(4)]
    xb = [lax.rem(x + 4 - d, 4) for d in range(4)]
    zs = [lax.rem(z + d, 4) for d in range(4)]
    ys = [lax.rem(yy + d, 4) for d in range(4)]
    sibling = device(h, oc, y, x, z)
    greet(
        [sibling, device(h, c, oy, x, z), device(oh, c, oy, x, z)]
        + [device(h, c, y, xs[d], z) for d in (1, 2, 3)]
        + [device(oh, c, y, xs[d], z) for d in (0, 1, 2, 3)]
        + [device(h, c, y, x, zs[d]) for d in (1, 2, 3)]
    )
    started = []

    def go(copy):
        copy.start()
        started.append(copy)
        return copy

    groups = (pl.ds(0, 4), pl.ds(4, 5))

    def x_slot(t, xv, hv):
        return x_all[t].at[:, pl.ds(pl.multiple_of(128 * (2 * xv + hv), 128), 128), :]

    def y_slot(t, zv, yv):
        return y_all[t].at[:, :, pl.ds(pl.multiple_of(128 * (2 * zv + yv), 128), 128)]

    across_h, across_y = device(oh, c, y, x, z), device(h, c, oy, x, z)
    ids_copy = go(remote(ids, id_all.at[h], (id_s, id_r), 0, across_h))
    firsts, got = [], ([], [])
    for t in range(2):
        x_part, y_part = x_mine.at[groups[t]], y_mine.at[groups[t]]
        firsts.append((
            go(remote(x_part, x_slot(t, x, h), (gx_s, gx_r), 8 * t, across_h)),
            go(remote(y_part, y_slot(t, z, y), (gy_s, gy_r), 8 * t, across_y)),
        ))
    for t in range(2):
        x_part, y_part = x_mine.at[groups[t]], y_mine.at[groups[t]]
        for d in (1, 3, 2):
            got[t].append(go(remote(x_part, x_slot(t, x, h), (gx_s, gx_r), 8 * t + d, device(h, c, y, xs[d], z))))
            got[t].append(go(remote(y_part, y_slot(t, z, y), (gy_s, gy_r), 8 * t + d, device(h, c, y, x, zs[d]))))
        for copy in firsts[t]:
            copy.wait_recv()
        for d in (1, 3, 2):
            got[t].append(go(remote(
                x_slot(t, x, oh), x_slot(t, x, oh), (gx_s, gx_r), 8 * t + 4 + d, device(h, c, y, xs[d], z))))
            got[t].append(go(remote(
                y_slot(t, z, oy), y_slot(t, z, oy), (gy_s, gy_r), 8 * t + 4 + d, device(h, c, y, x, zs[d]))))
    local = [pltpu.make_async_copy(ids, id_all.at[h], loc.at[2])]
    for t in range(2):
        local.append(pltpu.make_async_copy(x_mine.at[groups[t]], x_slot(t, x, h), loc.at[4 * t]))
        local.append(pltpu.make_async_copy(y_mine.at[groups[t]], y_slot(t, z, y), loc.at[1 + 4 * t]))
    for copy in local:
        copy.start()
    sq[...] = jnp.zeros_like(sq)
    acc[...] = jnp.zeros_like(acc)
    for copy in local:
        copy.wait()
    ids_copy.wait_recv()
    for g in range(2):
        row = id_all[g]
        for e in range(EX):
            first = jnp.sum((row < e).astype(jnp.int32))
            blks[8 * g + e] = jnp.minimum(first // 128, 2)

    def quarter(kt, group):
        rows = pl.ds(pl.multiple_of(256 * kt, 256), 256)

        def pairs(m, _):
            lefts, blocks = [], []
            for u in range(4):
                n = 4 * m + u
                e = n - 8 * group
                blk = blks[n]
                parts = []
                for b in range(2):
                    keep = id_all[group, blk + b] == e
                    parts.append(jnp.where(keep, x_all[group][blk + b, rows, :].astype(F32), 0.0).astype(BF16))
                lefts.append(jnp.concatenate(parts, axis=1))
                blocks.append(blk)
            for it in range(4):
                cols = pl.ds(256 * it, 256)
                total = sq[kt, :, cols]
                for u in range(4):
                    right = jnp.concatenate([y_all[group][blocks[u], :, cols], y_all[group][blocks[u] + 1, :, cols]], axis=0)
                    value = jnp.dot(lefts[u], right, preferred_element_type=F32).astype(BF16)
                    rot[4 * m + u, rows, cols] = value
                    wide = value.astype(F32)
                    total = total + wide * wide
                sq[kt, :, cols] = total
            return 0

        lax.fori_loop(2 * group, 2 * group + 2, pairs, 0)

    def sq_copy(kt):
        return remote(sq.at[kt], sq_got.at[kt], (sq_s, sq_r), kt, sibling)

    def add_up(kt):
        sq_copy(kt).wait()

        def chunk(i, _):
            part = pl.ds(pl.multiple_of(32 * i, 32), 32)
            sq[kt, part, :] = (sq[kt, part, :] + sq_got[kt, part, :]) * (1.0 / 32.0)
            return 0

        lax.fori_loop(0, 8, chunk, 0)
        c_stage[kt] = sq[kt, pl.ds(pl.multiple_of(128 * c, 128), 128), :].astype(BF16)

    def norms(g, total):
        wide_ids = [jnp.broadcast_to(id_all[g, b].astype(F32), (128, 128)) for b in range(4)]
        tall_ids = [wide.T for wide in wide_ids]
        for a in range(4):
            for b in range(4):
                part = pl.ds(128 * b, 128)
                if abs(a - b) > 1:
                    gram[0, pl.ds(128 * a, 128), part] = jnp.zeros((128, 128), BF16)
                    gram[1, pl.ds(128 * a, 128), part] = jnp.zeros((128, 128), BF16)
                    continue
                value = lax.dot_general(
                    y_all[g][a], y_all[g][b], (((1,), (1,)), ((), ())), preferred_element_type=F32)
                value = jnp.where(tall_ids[a] == wide_ids[b], value, 0.0)
                high = value.astype(BF16)
                gram[0, pl.ds(128 * a, 128), part] = high
                gram[1, pl.ds(128 * a, 128), part] = (value - high.astype(F32)).astype(BF16)

        def chunk(i, total):
            rows = pl.ds(pl.multiple_of(256 * i, 256), 256)
            left = jnp.concatenate([x_all[g][b, rows, :] for b in range(4)], axis=1)
            value = jnp.dot(left, gram[0], preferred_element_type=F32)
            value += jnp.dot(left, gram[1], preferred_element_type=F32)
            value = value * left.astype(F32)
            for b in range(4):
                total = total + jnp.sum(value[:, 128 * b:128 * b + 128].reshape(32, 8, 128), axis=0)
            return total

        return lax.fori_loop(0, 4, chunk, total)

    def slab(xv, hv):
        return corr.at[2 * xv + hv, pl.ds(pl.multiple_of(128 * c, 128), 128), :]

    def out_copies(j):
        copies = []
        for hd in range(2):
            if hd or j:
                copies.append(pltpu.make_async_remote_copy(
                    src_ref=c_stage.at[xs[j]], dst_ref=slab(x, h), send_sem=o_s.at[4 * hd + j],
                    recv_sem=o_r.at[4 * hd + j], device_id=device((h, oh)[hd], c, y, xs[j], z),
                    device_id_type=MESH))
        return copies

    own_out = pltpu.make_async_copy(c_stage.at[x], slab(x, h), loc.at[3])
    def at_y(v):
        return device(v // 2, c, lax.rem(v, 2), x, z)

    def over_x(d):
        return device(h, c, y, xs[d], z)

    def over_y(d):
        return at_y(ys[d])

    def over_z(d):
        return device(h, c, y, x, zs[d])

    def over_cores(d):
        return sibling

    class Spread:
        def __init__(self, value, axes, buf, got_buf, sems):
            self.value, self.axes, self.buf, self.got, self.sems, self.n = value, list(axes), buf, got_buf, sems, 0

        def start(self):
            n, (where, count) = self.n, self.axes[self.n]
            self.buf[n] = self.value
            self.copies = [
                go(remote(self.buf.at[n], self.got.at[n, d], self.sems, 3 * n + d, where(d + 1)))
                for d in range(count)]

        def wait(self):
            self.value = self.buf[self.n]
            for d, copy in enumerate(self.copies):
                copy.wait_recv()
                self.value = self.value + self.got[self.n, d]
            self.n += 1

    for copy in got[0]:
        copy.wait_recv()
    total = norms(0, jnp.zeros((8, 128), F32))
    for j in range(4):
        quarter(xs[j], 0)
    for copy in got[1]:
        copy.wait_recv()
    total = norms(1, total)
    whole = Spread(total, ((over_cores, 1), (over_x, 3), (over_y, 3), (over_z, 3)), red, red_got, (t_s, t_r))
    for j in range(4):
        whole.start()
        quarter(xs[j], 1)
        sq_copy(xs[j]).start()
        whole.wait()
        if j:
            add_up(xs[j - 1])
            for copy in out_copies(j - 1):
                copy.start()
            if j == 1:
                own_out.start()
    add_up(xs[3])
    for copy in out_copies(3):
        copy.start()
    damping = 0.5 * (jnp.sum(whole.value) * (1.0 / 32.0) / (float(D_IN) * float(D_OUT)))

    def second(kt):
        rows = pl.ds(pl.multiple_of(256 * kt, 256), 256)

        def invert(i, _):
            part = pl.ds(pl.multiple_of(32 * i, 32), 32)
            sq[kt, part, :] = 1.0 / (sq[kt, part, :] + damping)
            return 0

        lax.fori_loop(0, 8, invert, 0)

        def pairs(m, _):
            query_in = x_all[1][4, rows, :].astype(F32)
            sums = [None] * 4
            for it in range(4):
                cols = pl.ds(256 * it, 256)
                factor = sq[kt, :, cols]
                query_out = y_all[1][4, :, cols]
                for u in range(4):
                    cond = (rot[4 * m + u, rows, cols].astype(F32) * factor).astype(BF16)
                    part = lax.dot_general(
                        cond, query_out, (((1,), (1,)), ((), ())), preferred_element_type=F32)
                    sums[u] = part if it == 0 else sums[u] + part
            for u in range(4):
                acc[pl.ds(4 * m + u, 1), :] += jnp.sum(sums[u] * query_in, axis=0, keepdims=True)
            return 0

        lax.fori_loop(0, EX // 2, pairs, 0)

    def hand_on(xv, hv):
        return remote(slab(xv, hv), slab(xv, hv), (f_s, f_r), 2 * xv + hv, sibling)

    for j in range(4):
        second(xs[j])
        for copy in out_copies(j):
            copy.wait()
        if j == 0:
            own_out.wait()
        for hv in (h, oh):
            hand_on(xb[j], hv).start()
    result = Spread(acc[...], ((over_z, 3), (over_x, 3), (over_y, 3)), red2, red2_got, (p_s, p_r))
    for _ in range(3):
        result.start()
        result.wait()
    scores[...] = result.value
    for j in range(4):
        for hv in (h, oh):
            hand_on(xb[j], hv).wait()
    for copy in started:
        copy.wait_send()


def score(x_mine, y_mine, ids):
    dma = pltpu.SemaphoreType.DMA
    vmem = pl.BlockSpec(memory_space=pltpu.VMEM)
    return pl.pallas_call(
        score_kernel,
        out_shape=(jax.ShapeDtypeStruct((8, 256, 1024), BF16), jax.ShapeDtypeStruct((2 * EX, 128), F32)),
        in_specs=[vmem] * 3,
        out_specs=(pl.BlockSpec(memory_space=pltpu.VMEM), vmem),
        scratch_shapes=[
            (pltpu.VMEM((4, 1024, 128), BF16), pltpu.VMEM((5, 1024, 128), BF16)),
            (pltpu.VMEM((4, 128, 1024), BF16), pltpu.VMEM((5, 128, 1024), BF16)),
            pltpu.VMEM((2, 4, 1, 128), jnp.int32),
            pltpu.VMEM((2 * EX, 1024, 1024), BF16),
            pltpu.VMEM((4, 256, 1024), F32),
            pltpu.VMEM((4, 256, 1024), F32),
            pltpu.VMEM((4, 128, 1024), BF16),
            pltpu.VMEM((2 * EX, 128), F32),
            pltpu.VMEM((2, 512, 512), BF16),
            pltpu.VMEM((4, 8, 128), F32),
            pltpu.VMEM((4, 3, 8, 128), F32),
            pltpu.VMEM((3, 2 * EX, 128), F32),
            pltpu.VMEM((3, 3, 2 * EX, 128), F32),
            pltpu.SMEM((2 * EX,), jnp.int32),
            dma((6,)),
            dma((16,)), dma((16,)),
            dma((16,)), dma((16,)),
            dma((1,)), dma((1,)),
            dma((4,)), dma((4,)),
            dma((12,)), dma((12,)),
            dma((8,)), dma((8,)),
            dma((8,)), dma((8,)),
            dma((9,)), dma((9,)),
        ],
        compiler_params=pltpu.CompilerParams(
            collective_id=2, has_side_effects=True, vmem_limit_bytes=60 * 2**20),
        cost_estimate=pl.CostEstimate(flops=2 * 10**10, bytes_accessed=10**7, transcendentals=0),
        name="score",
    )(x_mine, y_mine, ids)


def widen_kernel(corr, out, stage, sems):
    def copy(n):
        yv, xv = n // 4, n % 4
        return pltpu.make_async_copy(stage.at[n % 4], out.at[:, pl.ds(1024 * (4 * yv + xv), 1024)], sems.at[n % 4])

    for n in range(8):
        yv, xv = n // 4, n % 4
        if n >= 4:
            copy(n - 4).wait()
        for zv in range(4):
            for hv in range(2):
                stage[n % 4, :, pl.ds(128 * (2 * zv + hv), 128)] = corr[
                    2 * xv + hv, :, pl.ds(128 * (2 * zv + yv), 128)].astype(F32)
        copy(n).start()
    for n in range(4, 8):
        copy(n).wait()


def widen(corr):
    return pl.pallas_call(
        widen_kernel,
        out_shape=jax.ShapeDtypeStruct((256, D_OUT), F32),
        in_specs=[pl.BlockSpec(memory_space=pltpu.VMEM)],
        out_specs=pl.BlockSpec(memory_space=pl.ANY),
        scratch_shapes=[pltpu.VMEM((4, 256, 1024), F32), pltpu.SemaphoreType.DMA((4,))],
        compiler_params=pltpu.CompilerParams(vmem_limit_bytes=60 * 2**20),
        name="widen",
    )(corr)


def per_device(activations, out_grads, query_acts, query_grads, eig_in, eig_out, example_ids):
    x_mine, y_mine = rotate(activations, out_grads, query_acts, query_grads, eig_in, eig_out)
    corr, sums = score(x_mine, y_mine, example_ids.reshape(4, 1, 128))
    h = lax.axis_index("dp") // 2
    mine = lax.dynamic_slice_in_dim(sums, EX * h, EX, 0)
    norm_factor = 1.0 / jnp.sqrt(jnp.float32(D_IN) * jnp.float32(D_OUT))
    scores = jnp.sum(mine.reshape(EX, NQ, QTOK), axis=2).T * norm_factor
    return widen(corr), scores


def solution(mesh):
    return jax.shard_map(
        per_device,
        mesh=mesh,
        in_specs=(
            P("dp", "fsdp"),
            P("dp", "fsdp"),
            P(None, "fsdp"),
            P(None, "fsdp"),
            P("fsdp", None),
            P("fsdp", None),
            P("dp", None),
        ),
        out_specs=(P("fsdp", None), P(None, "dp")),
        check_vma=False,
    )
```

```python
import jax
import jax.numpy as jnp
from jax import lax
from jax.experimental import pallas as pl
from jax.experimental.pallas import tpu as pltpu
from jax.sharding import PartitionSpec as P

D_IN = 8192
D_OUT = 8192
EX = 8
NQ = 32
QTOK = 4
ROWS = 1152
MESH = pl.DeviceIdType.MESH
F32 = jnp.float32
BF16 = jnp.bfloat16


def place():
    dp, fs = lax.axis_index("dp"), lax.axis_index("fsdp")
    return dp // 2, lax.rem(dp, 2), fs // 16, lax.rem(fs // 4, 4), lax.rem(fs, 4)


def device(h, c, y, x, z):
    return (2 * h + c, 16 * y + 4 * x + z)


def greet(partners):
    barrier = pltpu.get_barrier_semaphore()
    for partner in partners:
        pl.semaphore_signal(barrier, 1, device_id=partner, device_id_type=MESH)
    pl.semaphore_wait(barrier, len(partners))


def remote(src, dst, sems, slot, target):
    return pltpu.make_async_remote_copy(
        src_ref=src, dst_ref=dst, send_sem=sems[0].at[slot], recv_sem=sems[1].at[slot],
        device_id=target, device_id_type=MESH,
    )


def rotate_kernel(
    act, grd, qa, qg, eig_in, eig_out, x_out, y_out,
    a_buf, g_buf, u_buf, v_buf, in_bufs, out_bufs,
    loc, h_s, h_r, ag_s, ag_r, gg_s, gg_r, u_s, u_r, v_s, v_r, us_s, us_r, vsib_s, vsib_r,
    in_sems, out_sems,
):
    h, c, y, x, z = place()
    oh, oc, oy = 1 - h, 1 - c, 1 - y
    xs = [lax.rem(x + d, 4) for d in range(4)]
    zs = [lax.rem(z + d, 4) for d in range(4)]
    sibling = device(h, oc, y, x, z)
    partner = device(h, c, oy, x, z)
    greet(
        [sibling, device(oh, c, y, x, z), partner]
        + [device(h, c, y, xs[d], z) for d in (1, 2, 3)]
        + [device(h, c, y, x, zs[d]) for d in (1, 2, 3)]
        + [device(h, c, oy, x, zs[d]) for d in (1, 2, 3)]
    )
    started = []

    def go(copy):
        copy.start()
        started.append(copy)
        return copy

    ah = go(remote(act, a_buf.at[z, pl.ds(640, 512)], (h_s, h_r), 0, device(oh, c, y, x, z)))
    gh = go(remote(grd, g_buf.at[x, pl.ds(640, 512)], (h_s, h_r), 1, device(oh, c, y, x, z)))
    local = [
        pltpu.make_async_copy(act, a_buf.at[z, pl.ds(0, 512)], loc.at[0]),
        pltpu.make_async_copy(qa, a_buf.at[z, pl.ds(512, 128)], loc.at[1]),
        pltpu.make_async_copy(grd, g_buf.at[x, pl.ds(0, 512)], loc.at[2]),
        pltpu.make_async_copy(qg, g_buf.at[x, pl.ds(512, 128)], loc.at[3]),
    ]
    for copy in local:
        copy.start()
    u1 = []
    for d in (1, 3, 2):
        for p in range(4):
            u1.append(go(remote(
                eig_in.at[:, pl.ds(256 * (16 * c + 4 * p + zs[d]) + 128 * h, 128)],
                u_buf.at[z, p, :, pl.ds(128 * c, 128)],
                (u_s, u_r), 4 * d + p, device(h, c, y, x, zs[d]))))
    for copy in local:
        copy.wait()
    mine, other = pl.ds(0, 640), pl.ds(640, 512)
    a1, g1, a2, g2 = [], [], [], []
    for d in (1, 3, 2):
        a1.append(go(remote(a_buf.at[z, mine], a_buf.at[z, mine], (ag_s, ag_r), d, device(h, c, y, x, zs[d]))))
        g1.append(go(remote(g_buf.at[x, mine], g_buf.at[x, mine], (gg_s, gg_r), d, device(h, c, y, xs[d], z))))
    own = []
    for p in range(4):
        for q in range(2):
            own.append(pltpu.make_async_copy(
                eig_in.at[:, pl.ds(256 * (16 * q + 4 * p + z) + 128 * h, 128)],
                u_buf.at[z, p, :, pl.ds(128 * q, 128)], loc.at[12 + 2 * p + q]))
        own.append(pltpu.make_async_copy(
            eig_out.at[pl.ds(128 * h, 128), pl.ds(256 * (16 * y + 4 * p + z), 256)],
            v_buf.at[z, p, pl.ds(128 * y, 128)], loc.at[8 + p]))
    for copy in own:
        copy.start()
    ah.wait_recv()
    gh.wait_recv()
    for d in (1, 3, 2):
        a2.append(go(remote(a_buf.at[z, other], a_buf.at[z, other], (ag_s, ag_r), 4 + d, device(h, c, y, x, zs[d]))))
        g2.append(go(remote(g_buf.at[x, other], g_buf.at[x, other], (gg_s, gg_r), 4 + d, device(h, c, y, xs[d], z))))
    handed = []
    for n, d in enumerate((1, 3, 2)):
        src = lax.rem(z + 4 - d, 4)
        for p in range(4):
            u1[4 * n + p].wait_recv()
        part = u_buf.at[src, :, :, pl.ds(128 * c, 128)]
        handed.append(go(remote(part, part, (us_s, us_r), d, sibling)))
    for copy in own:
        copy.wait()
    for copy in a1:
        copy.wait_recv()
    v1 = []
    for dy, yd in ((1, oy), (0, y)):
        for d in (1, 3, 2, 0):
            if dy == 0 and d == 0:
                continue
            for p in range(2):
                piece = 2 * c + p
                v1.append((dy, d, p, go(remote(
                    eig_out.at[pl.ds(128 * h, 128), pl.ds(256 * (16 * yd + 4 * piece + zs[d]), 256)],
                    v_buf.at[z, piece, pl.ds(128 * y, 128)],
                    (v_s, v_r), 8 * dy + 2 * d + p, device(h, c, yd, x, zs[d])))))
    for copy in handed:
        copy.wait_recv()

    def halves(total):
        low, high = total[:, :128], total[:, 128:]
        return jnp.where(y == 0, low, high), jnp.where(y == 0, high, low)

    def rows_loop(first, count, tile, body):
        def step(i, _):
            start = pl.multiple_of(i * tile, tile)
            body(pl.ds(start, tile), pl.ds(pl.multiple_of(first + start, 64), tile))
            return 0
        lax.fori_loop(0, count // tile, step, 0)

    def side(product, bufs, sems, ring, coords):
        r_send, r_got, r_own, q_send, q_got, p_send, p_got, p_own, w_send, w_got, w_own = bufs
        r_s, r_r, w_s, w_r, y_s, y_r = sems
        sent = {}

        def ring_first():
            sent["ring"] = []
            for n, d in enumerate((1, 3, 2, 0)):
                if d:
                    def body(rows, src):
                        r_send[n, rows, :] = product(src, coords[d], 320).astype(BF16)
                    rows_loop(0, 640, 320, body)
                    sent["ring"].append(go(remote(r_send.at[n], r_got.at[n], (r_s, r_r), n, ring(d))))
                else:
                    def body(rows, src):
                        r_own[rows, :] = product(src, coords[0], 320)
                    rows_loop(0, 640, 320, body)

        def partner_first():
            for d in range(4):
                def body(rows, src):
                    keep, give = halves(product(src, coords[d], 256))
                    p_own[d, rows, :] = keep
                    p_send[coords[d], rows, :] = give.astype(BF16)
                rows_loop(640, 512, 256, body)
            sent["partner"] = go(remote(p_send, p_got, (y_s, y_r), 0, partner))

        def partner_then_ring():
            sent["partner"].wait_recv()
            sent["late"] = []
            for n, d in enumerate((1, 3, 2, 0)):
                def body(rows, _):
                    total = p_own[d, rows, :] + p_got[coords[d], rows, :].astype(F32)
                    if d:
                        w_send[n, rows, :] = total.astype(BF16)
                    else:
                        w_own[rows, :] = total
                rows_loop(0, 512, 256, body)
                if d:
                    sent["late"].append(go(remote(w_send.at[n], w_got.at[n], (w_s, w_r), n, ring(d))))

        def ring_then_partner():
            for copy in sent["ring"]:
                copy.wait_recv()

            def body(rows, _):
                total = r_own[rows, :]
                for n in range(3):
                    total += r_got[n, rows, :].astype(F32)
                r_own[rows, :] = total
                q_send[rows, :] = halves(total)[1].astype(BF16)
            rows_loop(0, 640, 128, body)
            sent["last"] = go(remote(q_send, q_got, (y_s, y_r), 1, partner))

        def finish(out, turn):
            for copy in sent["late"]:
                copy.wait_recv()

            def late(i, _):
                rows = pl.ds(pl.multiple_of(i * 128, 128), 128)
                total = w_own[rows, :]
                for n in range(3):
                    total += w_got[n, rows, :].astype(F32)
                out[4 * oh + i] = (total.T if turn else total).astype(BF16)
                return 0
            lax.fori_loop(0, 4, late, 0)
            sent["last"].wait_recv()

            def first(i, _):
                rows = pl.ds(pl.multiple_of(i * 128, 128), 128)
                total = halves(r_own[rows, :])[0] + q_got[rows, :].astype(F32)
                out[jnp.where(i < 4, 4 * h + i, 8)] = (total.T if turn else total).astype(BF16)
                return 0
            lax.fori_loop(0, 5, first, 0)

        return ring_first, partner_first, partner_then_ring, ring_then_partner, finish

    def product_in(rows, piece, tile):
        total = jnp.zeros((tile, 256), F32)
        for s in range(4):
            total += jnp.dot(a_buf[s, rows, :], u_buf[s, piece], preferred_element_type=F32)
        return total

    def product_out(rows, piece, tile):
        total = jnp.zeros((tile, 256), F32)
        for s in range(4):
            total += lax.dot_general(
                g_buf[s, rows, :], v_buf[piece, s], (((1,), (1,)), ((), ())), preferred_element_type=F32)
        return total

    in_side = side(product_in, in_bufs, in_sems, lambda d: device(h, c, y, xs[d], z), xs)
    out_side = side(product_out, out_bufs, out_sems, lambda d: device(h, c, y, x, zs[d]), zs)
    in_side[0]()
    for copy in a2:
        copy.wait_recv()
    in_side[1]()
    vhanded = []
    for n in range(len(v1) // 2):
        dy, d, _, copy = v1[2 * n]
        copy.wait_recv()
        v1[2 * n + 1][3].wait_recv()
        src = lax.rem(z + 4 - d, 4)
        part = v_buf.at[src, pl.ds(2 * c, 2), pl.ds(128 * (oy if dy else y), 128)]
        vhanded.append(go(remote(part, part, (vsib_s, vsib_r), 4 * dy + d, sibling)))
    for copy in g1 + g2 + vhanded:
        copy.wait_recv()
    out_side[1]()
    out_side[0]()
    in_side[2]()
    in_side[3]()
    out_side[2]()
    out_side[3]()
    in_side[4](x_out, True)
    out_side[4](y_out, False)
    for copy in started:
        copy.wait_send()


def rotate(act, grd, qa, qg, eig_in, eig_out):
    dma = pltpu.SemaphoreType.DMA
    any_ = pl.BlockSpec(memory_space=pl.ANY)
    vmem = pl.BlockSpec(memory_space=pltpu.VMEM)

    def side_bufs():
        return (
            pltpu.VMEM((3, 640, 256), BF16), pltpu.VMEM((3, 640, 256), BF16), pltpu.VMEM((640, 256), F32),
            pltpu.VMEM((640, 128), BF16), pltpu.VMEM((640, 128), BF16),
            pltpu.VMEM((4, 512, 128), BF16), pltpu.VMEM((4, 512, 128), BF16), pltpu.VMEM((4, 512, 128), F32),
            pltpu.VMEM((3, 512, 128), BF16), pltpu.VMEM((3, 512, 128), BF16), pltpu.VMEM((512, 128), F32),
        )

    def side_sems():
        return tuple([dma((3,))] * 4 + [dma((2,))] * 2)

    return pl.pallas_call(
        rotate_kernel,
        out_shape=(jax.ShapeDtypeStruct((9, 128, 128), BF16), jax.ShapeDtypeStruct((9, 128, 128), BF16)),
        in_specs=[any_] * 6,
        out_specs=(vmem, vmem),
        scratch_shapes=[
            pltpu.VMEM((4, ROWS, 256), BF16),
            pltpu.VMEM((4, ROWS, 256), BF16),
            pltpu.VMEM((4, 4, 256, 256), BF16),
            pltpu.VMEM((4, 4, 256, 256), BF16),
            side_bufs(), side_bufs(),
            dma((20,)),
            dma((2,)), dma((2,)),
            dma((8,)), dma((8,)),
            dma((8,)), dma((8,)),
            dma((16,)), dma((16,)),
            dma((16,)), dma((16,)),
            dma((4,)), dma((4,)),
            dma((8,)), dma((8,)),
            side_sems(), side_sems(),
        ],
        compiler_params=pltpu.CompilerParams(
            collective_id=1, has_side_effects=True, vmem_limit_bytes=60 * 2**20),
        cost_estimate=pl.CostEstimate(flops=5 * 10**9, bytes_accessed=10**7, transcendentals=0),
        name="rotate",
    )(act, grd, qa, qg, eig_in, eig_out)


def score_kernel(
    x_mine, y_mine, ids, corr, scores,
    x_all, y_all, id_all, rot, sq, sq_got, c_stage, acc, gram, red, red_got, red2, red2_got, blks,
    loc, gx_s, gx_r, gy_s, gy_r, id_s, id_r, sq_s, sq_r, t_s, t_r, o_s, o_r, f_s, f_r, p_s, p_r,
):
    h, c, y, x, z = place()
    oh, oc, oy = 1 - h, 1 - c, 1 - y
    yy = 2 * h + y
    xs = [lax.rem(x + d, 4) for d in range(4)]
    xb = [lax.rem(x + 4 - d, 4) for d in range(4)]
    zs = [lax.rem(z + d, 4) for d in range(4)]
    ys = [lax.rem(yy + d, 4) for d in range(4)]
    sibling = device(h, oc, y, x, z)
    greet(
        [sibling, device(h, c, oy, x, z), device(oh, c, oy, x, z)]
        + [device(h, c, y, xs[d], z) for d in (1, 2, 3)]
        + [device(oh, c, y, x, z)]
        + [device(h, c, y, x, zs[d]) for d in (1, 2, 3)]
    )
    started = []

    def go(copy):
        copy.start()
        started.append(copy)
        return copy

    groups = (pl.ds(0, 4), pl.ds(4, 5))

    def x_slot(t, xv, hv):
        return x_all[t].at[:, pl.ds(pl.multiple_of(128 * (2 * xv + hv), 128), 128), :]

    def y_slot(t, zv, yv):
        return y_all[t].at[:, :, pl.ds(pl.multiple_of(128 * (2 * zv + yv), 128), 128)]

    across_h, across_y = device(oh, c, y, x, z), device(h, c, oy, x, z)
    ids_copy = go(remote(ids, id_all.at[h], (id_s, id_r), 0, across_h))
    firsts, got = [], ([], [])
    for t in range(2):
        x_part, y_part = x_mine.at[groups[t]], y_mine.at[groups[t]]
        firsts.append((
            go(remote(x_part, x_slot(t, x, h), (gx_s, gx_r), 8 * t, across_h)),
            go(remote(y_part, y_slot(t, z, y), (gy_s, gy_r), 8 * t, across_y)),
        ))
    for t in range(2):
        x_part, y_part = x_mine.at[groups[t]], y_mine.at[groups[t]]
        for d in (1, 3, 2):
            got[t].append(go(remote(x_part, x_slot(t, x, h), (gx_s, gx_r), 8 * t + d, device(h, c, y, xs[d], z))))
            got[t].append(go(remote(y_part, y_slot(t, z, y), (gy_s, gy_r), 8 * t + d, device(h, c, y, x, zs[d]))))
        for copy in firsts[t]:
            copy.wait_recv()
        for d in (1, 3, 2):
            got[t].append(go(remote(
                x_slot(t, x, oh), x_slot(t, x, oh), (gx_s, gx_r), 8 * t + 4 + d, device(h, c, y, xs[d], z))))
            got[t].append(go(remote(
                y_slot(t, z, oy), y_slot(t, z, oy), (gy_s, gy_r), 8 * t + 4 + d, device(h, c, y, x, zs[d]))))
    local = [pltpu.make_async_copy(ids, id_all.at[h], loc.at[2])]
    for t in range(2):
        local.append(pltpu.make_async_copy(x_mine.at[groups[t]], x_slot(t, x, h), loc.at[4 * t]))
        local.append(pltpu.make_async_copy(y_mine.at[groups[t]], y_slot(t, z, y), loc.at[1 + 4 * t]))
    for copy in local:
        copy.start()
    sq[...] = jnp.zeros_like(sq)
    acc[...] = jnp.zeros_like(acc)
    for copy in local:
        copy.wait()
    ids_copy.wait_recv()
    for g in range(2):
        row = id_all[g]
        for e in range(EX):
            first = jnp.sum((row < e).astype(jnp.int32))
            blks[8 * g + e] = jnp.minimum(first // 128, 2)

    def quarter(kt, group):
        rows = pl.ds(pl.multiple_of(256 * kt, 256), 256)

        def pairs(m, _):
            lefts, blocks = [], []
            for u in range(4):
                n = 4 * m + u
                e = n - 8 * group
                blk = blks[n]
                parts = []
                for b in range(2):
                    keep = id_all[group, blk + b] == e
                    parts.append(jnp.where(keep, x_all[group][blk + b, rows, :].astype(F32), 0.0).astype(BF16))
                lefts.append(jnp.concatenate(parts, axis=1))
                blocks.append(blk)
            for it in range(4):
                cols = pl.ds(256 * it, 256)
                total = sq[kt, :, cols]
                for u in range(4):
                    right = jnp.concatenate([y_all[group][blocks[u], :, cols], y_all[group][blocks[u] + 1, :, cols]], axis=0)
                    value = jnp.dot(lefts[u], right, preferred_element_type=F32).astype(BF16)
                    rot[4 * m + u, rows, cols] = value
                    wide = value.astype(F32)
                    total = total + wide * wide
                sq[kt, :, cols] = total
            return 0

        lax.fori_loop(2 * group, 2 * group + 2, pairs, 0)

    def sq_copy(kt):
        return remote(sq.at[kt], sq_got.at[kt], (sq_s, sq_r), kt, sibling)

    def add_up(kt):
        sq_copy(kt).wait()

        def chunk(i, _):
            part = pl.ds(pl.multiple_of(32 * i, 32), 32)
            sq[kt, part, :] = (sq[kt, part, :] + sq_got[kt, part, :]) * (1.0 / 32.0)
            return 0

        lax.fori_loop(0, 8, chunk, 0)
        c_stage[kt] = sq[kt, pl.ds(pl.multiple_of(128 * c, 128), 128), :].astype(BF16)

    def norms(g, total):
        wide_ids = [jnp.broadcast_to(id_all[g, b].astype(F32), (128, 128)) for b in range(4)]
        tall_ids = [wide.T for wide in wide_ids]
        for a in range(4):
            for b in range(4):
                part = pl.ds(128 * b, 128)
                if abs(a - b) > 1:
                    gram[0, pl.ds(128 * a, 128), part] = jnp.zeros((128, 128), BF16)
                    gram[1, pl.ds(128 * a, 128), part] = jnp.zeros((128, 128), BF16)
                    continue
                value = lax.dot_general(
                    y_all[g][a], y_all[g][b], (((1,), (1,)), ((), ())), preferred_element_type=F32)
                value = jnp.where(tall_ids[a] == wide_ids[b], value, 0.0)
                high = value.astype(BF16)
                gram[0, pl.ds(128 * a, 128), part] = high
                gram[1, pl.ds(128 * a, 128), part] = (value - high.astype(F32)).astype(BF16)

        def chunk(i, total):
            rows = pl.ds(pl.multiple_of(256 * i, 256), 256)
            left = jnp.concatenate([x_all[g][b, rows, :] for b in range(4)], axis=1)
            value = jnp.dot(left, gram[0], preferred_element_type=F32)
            value += jnp.dot(left, gram[1], preferred_element_type=F32)
            value = value * left.astype(F32)
            for b in range(4):
                total = total + jnp.sum(value[:, 128 * b:128 * b + 128].reshape(32, 8, 128), axis=0)
            return total

        return lax.fori_loop(0, 4, chunk, total)

    def slab(xv, hv):
        return corr.at[2 * xv + hv, pl.ds(pl.multiple_of(128 * c, 128), 128), :]

    def out_copy(j):
        return remote(c_stage.at[xs[j]], slab(x, h), (o_s, o_r), j, device(h, c, y, xs[j], z))

    def cross(j):
        src = slab(xb[j], h) if j else c_stage.at[x]
        return remote(src, slab(xb[j], h), (o_s, o_r), 4 + j, across_h)

    own_out = pltpu.make_async_copy(c_stage.at[x], slab(x, h), loc.at[3])
    def at_y(v):
        return device(v // 2, c, lax.rem(v, 2), x, z)

    def over_x(d):
        return device(h, c, y, xs[d], z)

    def over_y(d):
        return at_y(ys[d])

    def over_z(d):
        return device(h, c, y, x, zs[d])

    def over_cores(d):
        return sibling

    class Spread:
        def __init__(self, value, axes, buf, got_buf, sems):
            self.value, self.axes, self.buf, self.got, self.sems, self.n = value, list(axes), buf, got_buf, sems, 0

        def start(self):
            n, (where, count) = self.n, self.axes[self.n]
            self.buf[n] = self.value
            self.copies = [
                go(remote(self.buf.at[n], self.got.at[n, d], self.sems, 3 * n + d, where(d + 1)))
                for d in range(count)]

        def wait(self):
            self.value = self.buf[self.n]
            for d, copy in enumerate(self.copies):
                copy.wait_recv()
                self.value = self.value + self.got[self.n, d]
            self.n += 1

    for copy in got[0]:
        copy.wait_recv()
    total = norms(0, jnp.zeros((8, 128), F32))
    for j in range(4):
        quarter(xs[j], 0)
    for copy in got[1]:
        copy.wait_recv()
    total = norms(1, total)
    whole = Spread(total, ((over_cores, 1), (over_x, 3), (over_y, 3), (over_z, 3)), red, red_got, (t_s, t_r))
    for j in range(4):
        whole.start()
        quarter(xs[j], 1)
        sq_copy(xs[j]).start()
        whole.wait()
        if j:
            add_up(xs[j - 1])
            if j == 1:
                cross(0).start()
                own_out.start()
            else:
                out_copy(j - 1).start()
    add_up(xs[3])
    out_copy(3).start()
    damping = 0.5 * (jnp.sum(whole.value) * (1.0 / 32.0) / (float(D_IN) * float(D_OUT)))

    def second(kt):
        rows = pl.ds(pl.multiple_of(256 * kt, 256), 256)

        def invert(i, _):
            part = pl.ds(pl.multiple_of(32 * i, 32), 32)
            sq[kt, part, :] = 1.0 / (sq[kt, part, :] + damping)
            return 0

        lax.fori_loop(0, 8, invert, 0)

        def pairs(m, _):
            query_in = x_all[1][4, rows, :].astype(F32)
            sums = [None] * 4
            for it in range(4):
                cols = pl.ds(256 * it, 256)
                factor = sq[kt, :, cols]
                query_out = y_all[1][4, :, cols]
                for u in range(4):
                    cond = (rot[4 * m + u, rows, cols].astype(F32) * factor).astype(BF16)
                    part = lax.dot_general(
                        cond, query_out, (((1,), (1,)), ((), ())), preferred_element_type=F32)
                    sums[u] = part if it == 0 else sums[u] + part
            for u in range(4):
                acc[pl.ds(4 * m + u, 1), :] += jnp.sum(sums[u] * query_in, axis=0, keepdims=True)
            return 0

        lax.fori_loop(0, EX // 2, pairs, 0)

    def hand_on(xv, hv):
        return remote(slab(xv, hv), slab(xv, hv), (f_s, f_r), 2 * xv + hv, sibling)

    def pass_on(j):
        if j:
            out_copy(j).wait()
            cross(j).start()
        else:
            own_out.wait()
        hand_on(xb[j], h).start()

    def take(j):
        cross(j).wait()
        hand_on(xb[j], oh).start()

    pass_on(1)
    second(xs[0])
    pass_on(2)
    second(xs[1])
    pass_on(3)
    second(xs[2])
    pass_on(0)
    second(xs[3])
    result = Spread(acc[...], ((over_z, 3), (over_x, 3), (over_y, 3)), red2, red2_got, (p_s, p_r))
    result.start()
    take(0)
    result.wait()
    result.start()
    take(1)
    result.wait()
    result.start()
    take(2)
    result.wait()
    take(3)
    scores[...] = result.value
    for j in range(4):
        for hv in (h, oh):
            hand_on(xb[j], hv).wait()
    for copy in started:
        copy.wait_send()


def score(x_mine, y_mine, ids):
    dma = pltpu.SemaphoreType.DMA
    vmem = pl.BlockSpec(memory_space=pltpu.VMEM)
    return pl.pallas_call(
        score_kernel,
        out_shape=(jax.ShapeDtypeStruct((8, 256, 1024), BF16), jax.ShapeDtypeStruct((2 * EX, 128), F32)),
        in_specs=[vmem] * 3,
        out_specs=(pl.BlockSpec(memory_space=pltpu.VMEM), vmem),
        scratch_shapes=[
            (pltpu.VMEM((4, 1024, 128), BF16), pltpu.VMEM((5, 1024, 128), BF16)),
            (pltpu.VMEM((4, 128, 1024), BF16), pltpu.VMEM((5, 128, 1024), BF16)),
            pltpu.VMEM((2, 4, 1, 128), jnp.int32),
            pltpu.VMEM((2 * EX, 1024, 1024), BF16),
            pltpu.VMEM((4, 256, 1024), F32),
            pltpu.VMEM((4, 256, 1024), F32),
            pltpu.VMEM((4, 128, 1024), BF16),
            pltpu.VMEM((2 * EX, 128), F32),
            pltpu.VMEM((2, 512, 512), BF16),
            pltpu.VMEM((4, 8, 128), F32),
            pltpu.VMEM((4, 3, 8, 128), F32),
            pltpu.VMEM((3, 2 * EX, 128), F32),
            pltpu.VMEM((3, 3, 2 * EX, 128), F32),
            pltpu.SMEM((2 * EX,), jnp.int32),
            dma((6,)),
            dma((16,)), dma((16,)),
            dma((16,)), dma((16,)),
            dma((1,)), dma((1,)),
            dma((4,)), dma((4,)),
            dma((12,)), dma((12,)),
            dma((8,)), dma((8,)),
            dma((8,)), dma((8,)),
            dma((9,)), dma((9,)),
        ],
        compiler_params=pltpu.CompilerParams(
            collective_id=2, has_side_effects=True, vmem_limit_bytes=60 * 2**20),
        cost_estimate=pl.CostEstimate(flops=2 * 10**10, bytes_accessed=10**7, transcendentals=0),
        name="score",
    )(x_mine, y_mine, ids)


def widen_kernel(corr, out, stage, sems):
    def copy(n):
        yv, xv = n // 4, n % 4
        return pltpu.make_async_copy(stage.at[n % 4], out.at[:, pl.ds(1024 * (4 * yv + xv), 1024)], sems.at[n % 4])

    for n in range(8):
        yv, xv = n // 4, n % 4
        if n >= 4:
            copy(n - 4).wait()
        for zv in range(4):
            for hv in range(2):
                stage[n % 4, :, pl.ds(128 * (2 * zv + hv), 128)] = corr[
                    2 * xv + hv, :, pl.ds(128 * (2 * zv + yv), 128)].astype(F32)
        copy(n).start()
    for n in range(4, 8):
        copy(n).wait()


def widen(corr):
    return pl.pallas_call(
        widen_kernel,
        out_shape=jax.ShapeDtypeStruct((256, D_OUT), F32),
        in_specs=[pl.BlockSpec(memory_space=pltpu.VMEM)],
        out_specs=pl.BlockSpec(memory_space=pl.ANY),
        scratch_shapes=[pltpu.VMEM((4, 256, 1024), F32), pltpu.SemaphoreType.DMA((4,))],
        compiler_params=pltpu.CompilerParams(vmem_limit_bytes=60 * 2**20),
        name="widen",
    )(corr)


def per_device(activations, out_grads, query_acts, query_grads, eig_in, eig_out, example_ids):
    x_mine, y_mine = rotate(activations, out_grads, query_acts, query_grads, eig_in, eig_out)
    corr, sums = score(x_mine, y_mine, example_ids.reshape(4, 1, 128))
    h = lax.axis_index("dp") // 2
    mine = lax.dynamic_slice_in_dim(sums, EX * h, EX, 0)
    norm_factor = 1.0 / jnp.sqrt(jnp.float32(D_IN) * jnp.float32(D_OUT))
    scores = jnp.sum(mine.reshape(EX, NQ, QTOK), axis=2).T * norm_factor
    return widen(corr), scores


def solution(mesh):
    return jax.shard_map(
        per_device,
        mesh=mesh,
        in_specs=(
            P("dp", "fsdp"),
            P("dp", "fsdp"),
            P(None, "fsdp"),
            P(None, "fsdp"),
            P("fsdp", None),
            P("fsdp", None),
            P("dp", None),
        ),
        out_specs=(P("fsdp", None), P(None, "dp")),
        check_vma=False,
    )
```

```python
import jax
import jax.numpy as jnp
from jax import lax
from jax.experimental import pallas as pl
from jax.experimental.pallas import tpu as pltpu
from jax.sharding import PartitionSpec as P

D_IN = 8192
D_OUT = 8192
EX = 8
NQ = 32
QTOK = 4
ROWS = 1152
MESH = pl.DeviceIdType.MESH
F32 = jnp.float32
BF16 = jnp.bfloat16


def place():
    dp, fs = lax.axis_index("dp"), lax.axis_index("fsdp")
    return dp // 2, lax.rem(dp, 2), fs // 16, lax.rem(fs // 4, 4), lax.rem(fs, 4)


def device(h, c, y, x, z):
    return (2 * h + c, 16 * y + 4 * x + z)


def greet(partners):
    barrier = pltpu.get_barrier_semaphore()
    for partner in partners:
        pl.semaphore_signal(barrier, 1, device_id=partner, device_id_type=MESH)
    pl.semaphore_wait(barrier, len(partners))


def remote(src, dst, sems, slot, target):
    return pltpu.make_async_remote_copy(
        src_ref=src, dst_ref=dst, send_sem=sems[0].at[slot], recv_sem=sems[1].at[slot],
        device_id=target, device_id_type=MESH,
    )


def rotate_kernel(
    act, grd, qa, qg, eig_in, eig_out, x_out, y_out,
    a_buf, g_buf, u_buf, v_buf, in_bufs, out_bufs,
    loc, h_s, h_r, ag_s, ag_r, gg_s, gg_r, u_s, u_r, v_s, v_r, us_s, us_r, vsib_s, vsib_r,
    in_sems, out_sems,
):
    h, c, y, x, z = place()
    oh, oc, oy = 1 - h, 1 - c, 1 - y
    xs = [lax.rem(x + d, 4) for d in range(4)]
    zs = [lax.rem(z + d, 4) for d in range(4)]
    sibling = device(h, oc, y, x, z)
    partner = device(h, c, oy, x, z)
    greet(
        [sibling, device(oh, c, y, x, z), partner]
        + [device(h, c, y, xs[d], z) for d in (1, 2, 3)]
        + [device(h, c, y, x, zs[d]) for d in (1, 2, 3)]
        + [device(h, c, oy, x, zs[d]) for d in (1, 2, 3)]
    )
    started = []

    def go(copy):
        copy.start()
        started.append(copy)
        return copy

    ah = go(remote(act, a_buf.at[z, pl.ds(640, 512)], (h_s, h_r), 0, device(oh, c, y, x, z)))
    gh = go(remote(grd, g_buf.at[x, pl.ds(640, 512)], (h_s, h_r), 1, device(oh, c, y, x, z)))
    local = [
        pltpu.make_async_copy(act, a_buf.at[z, pl.ds(0, 512)], loc.at[0]),
        pltpu.make_async_copy(qa, a_buf.at[z, pl.ds(512, 128)], loc.at[1]),
        pltpu.make_async_copy(grd, g_buf.at[x, pl.ds(0, 512)], loc.at[2]),
        pltpu.make_async_copy(qg, g_buf.at[x, pl.ds(512, 128)], loc.at[3]),
    ]
    for copy in local:
        copy.start()
    u1 = []
    for d in (1, 3, 2):
        for p in range(4):
            u1.append(go(remote(
                eig_in.at[:, pl.ds(256 * (16 * c + 4 * p + zs[d]) + 128 * h, 128)],
                u_buf.at[z, p, :, pl.ds(128 * c, 128)],
                (u_s, u_r), 4 * d + p, device(h, c, y, x, zs[d]))))
    for copy in local:
        copy.wait()
    mine, other = pl.ds(0, 640), pl.ds(640, 512)
    a1, g1, a2, g2 = [], [], [], []
    for d in (1, 3, 2):
        a1.append(go(remote(a_buf.at[z, mine], a_buf.at[z, mine], (ag_s, ag_r), d, device(h, c, y, x, zs[d]))))
        g1.append(go(remote(g_buf.at[x, mine], g_buf.at[x, mine], (gg_s, gg_r), d, device(h, c, y, xs[d], z))))
    own = []
    for p in range(4):
        for q in range(2):
            own.append(pltpu.make_async_copy(
                eig_in.at[:, pl.ds(256 * (16 * q + 4 * p + z) + 128 * h, 128)],
                u_buf.at[z, p, :, pl.ds(128 * q, 128)], loc.at[12 + 2 * p + q]))
        own.append(pltpu.make_async_copy(
            eig_out.at[pl.ds(128 * h, 128), pl.ds(256 * (16 * y + 4 * p + z), 256)],
            v_buf.at[z, p, pl.ds(128 * y, 128)], loc.at[8 + p]))
    for copy in own:
        copy.start()
    ah.wait_recv()
    gh.wait_recv()
    for d in (1, 3, 2):
        a2.append(go(remote(a_buf.at[z, other], a_buf.at[z, other], (ag_s, ag_r), 4 + d, device(h, c, y, x, zs[d]))))
        g2.append(go(remote(g_buf.at[x, other], g_buf.at[x, other], (gg_s, gg_r), 4 + d, device(h, c, y, xs[d], z))))
    handed = []
    for n, d in enumerate((1, 3, 2)):
        src = lax.rem(z + 4 - d, 4)
        for p in range(4):
            u1[4 * n + p].wait_recv()
        part = u_buf.at[src, :, :, pl.ds(128 * c, 128)]
        handed.append(go(remote(part, part, (us_s, us_r), d, sibling)))
    for copy in own:
        copy.wait()
    for copy in a1:
        copy.wait_recv()
    v1 = []
    for dy, yd in ((1, oy), (0, y)):
        for d in (1, 3, 2, 0):
            if dy == 0 and d == 0:
                continue
            for p in range(2):
                piece = 2 * c + p
                v1.append((dy, d, p, go(remote(
                    eig_out.at[pl.ds(128 * h, 128), pl.ds(256 * (16 * yd + 4 * piece + zs[d]), 256)],
                    v_buf.at[z, piece, pl.ds(128 * y, 128)],
                    (v_s, v_r), 8 * dy + 2 * d + p, device(h, c, yd, x, zs[d])))))
    for copy in handed:
        copy.wait_recv()

    def halves(total):
        low, high = total[:, :128], total[:, 128:]
        return jnp.where(y == 0, low, high), jnp.where(y == 0, high, low)

    def rows_loop(first, count, tile, body):
        def step(i, _):
            start = pl.multiple_of(i * tile, tile)
            body(pl.ds(start, tile), pl.ds(pl.multiple_of(first + start, 64), tile))
            return 0
        lax.fori_loop(0, count // tile, step, 0)

    def side(product, bufs, sems, ring, coords):
        r_send, r_got, r_own, q_send, q_got, p_send, p_got, p_own, w_send, w_got, w_own = bufs
        r_s, r_r, w_s, w_r, y_s, y_r = sems
        sent = {}

        def ring_first():
            sent["ring"] = []
            for n, d in enumerate((1, 3, 2, 0)):
                if d:
                    def body(rows, src):
                        r_send[n, rows, :] = product(src, coords[d], 320).astype(BF16)
                    rows_loop(0, 640, 320, body)
                    sent["ring"].append(go(remote(r_send.at[n], r_got.at[n], (r_s, r_r), n, ring(d))))
                else:
                    def body(rows, src):
                        r_own[rows, :] = product(src, coords[0], 320)
                    rows_loop(0, 640, 320, body)

        def partner_first():
            for d in range(4):
                def body(rows, src):
                    keep, give = halves(product(src, coords[d], 256))
                    p_own[d, rows, :] = keep
                    p_send[coords[d], rows, :] = give.astype(BF16)
                rows_loop(640, 512, 256, body)
            sent["partner"] = go(remote(p_send, p_got, (y_s, y_r), 0, partner))

        def partner_then_ring():
            sent["partner"].wait_recv()
            sent["late"] = []
            for n, d in enumerate((1, 3, 2, 0)):
                def body(rows, _):
                    total = p_own[d, rows, :] + p_got[coords[d], rows, :].astype(F32)
                    if d:
                        w_send[n, rows, :] = total.astype(BF16)
                    else:
                        w_own[rows, :] = total
                rows_loop(0, 512, 256, body)
                if d:
                    sent["late"].append(go(remote(w_send.at[n], w_got.at[n], (w_s, w_r), n, ring(d))))

        def ring_then_partner():
            for copy in sent["ring"]:
                copy.wait_recv()

            def body(rows, _):
                total = r_own[rows, :]
                for n in range(3):
                    total += r_got[n, rows, :].astype(F32)
                r_own[rows, :] = total
                q_send[rows, :] = halves(total)[1].astype(BF16)
            rows_loop(0, 640, 128, body)
            sent["last"] = go(remote(q_send, q_got, (y_s, y_r), 1, partner))

        def finish(out, turn):
            for copy in sent["late"]:
                copy.wait_recv()

            def late(i, _):
                rows = pl.ds(pl.multiple_of(i * 128, 128), 128)
                total = w_own[rows, :]
                for n in range(3):
                    total += w_got[n, rows, :].astype(F32)
                out[4 * oh + i] = (total.T if turn else total).astype(BF16)
                return 0
            lax.fori_loop(0, 4, late, 0)
            sent["last"].wait_recv()

            def first(i, _):
                rows = pl.ds(pl.multiple_of(i * 128, 128), 128)
                total = halves(r_own[rows, :])[0] + q_got[rows, :].astype(F32)
                out[jnp.where(i < 4, 4 * h + i, 8)] = (total.T if turn else total).astype(BF16)
                return 0
            lax.fori_loop(0, 5, first, 0)

        return ring_first, partner_first, partner_then_ring, ring_then_partner, finish

    def product_in(rows, piece, tile):
        total = jnp.zeros((tile, 256), F32)
        for s in range(4):
            total += jnp.dot(a_buf[s, rows, :], u_buf[s, piece], preferred_element_type=F32)
        return total

    def product_out(rows, piece, tile):
        total = jnp.zeros((tile, 256), F32)
        for s in range(4):
            total += lax.dot_general(
                g_buf[s, rows, :], v_buf[piece, s], (((1,), (1,)), ((), ())), preferred_element_type=F32)
        return total

    in_side = side(product_in, in_bufs, in_sems, lambda d: device(h, c, y, xs[d], z), xs)
    out_side = side(product_out, out_bufs, out_sems, lambda d: device(h, c, y, x, zs[d]), zs)
    in_side[0]()
    for copy in a2:
        copy.wait_recv()
    in_side[1]()
    vhanded = []
    for n in range(len(v1) // 2):
        dy, d, _, copy = v1[2 * n]
        copy.wait_recv()
        v1[2 * n + 1][3].wait_recv()
        src = lax.rem(z + 4 - d, 4)
        part = v_buf.at[src, pl.ds(2 * c, 2), pl.ds(128 * (oy if dy else y), 128)]
        vhanded.append(go(remote(part, part, (vsib_s, vsib_r), 4 * dy + d, sibling)))
    for copy in g1 + g2 + vhanded:
        copy.wait_recv()
    out_side[1]()
    out_side[0]()
    in_side[2]()
    in_side[3]()
    out_side[2]()
    out_side[3]()
    in_side[4](x_out, True)
    out_side[4](y_out, False)
    for copy in started:
        copy.wait_send()


def rotate(act, grd, qa, qg, eig_in, eig_out):
    dma = pltpu.SemaphoreType.DMA
    any_ = pl.BlockSpec(memory_space=pl.ANY)
    vmem = pl.BlockSpec(memory_space=pltpu.VMEM)

    def side_bufs():
        return (
            pltpu.VMEM((3, 640, 256), BF16), pltpu.VMEM((3, 640, 256), BF16), pltpu.VMEM((640, 256), F32),
            pltpu.VMEM((640, 128), BF16), pltpu.VMEM((640, 128), BF16),
            pltpu.VMEM((4, 512, 128), BF16), pltpu.VMEM((4, 512, 128), BF16), pltpu.VMEM((4, 512, 128), F32),
            pltpu.VMEM((3, 512, 128), BF16), pltpu.VMEM((3, 512, 128), BF16), pltpu.VMEM((512, 128), F32),
        )

    def side_sems():
        return tuple([dma((3,))] * 4 + [dma((2,))] * 2)

    return pl.pallas_call(
        rotate_kernel,
        out_shape=(jax.ShapeDtypeStruct((9, 128, 128), BF16), jax.ShapeDtypeStruct((9, 128, 128), BF16)),
        in_specs=[any_] * 6,
        out_specs=(vmem, vmem),
        scratch_shapes=[
            pltpu.VMEM((4, ROWS, 256), BF16),
            pltpu.VMEM((4, ROWS, 256), BF16),
            pltpu.VMEM((4, 4, 256, 256), BF16),
            pltpu.VMEM((4, 4, 256, 256), BF16),
            side_bufs(), side_bufs(),
            dma((20,)),
            dma((2,)), dma((2,)),
            dma((8,)), dma((8,)),
            dma((8,)), dma((8,)),
            dma((16,)), dma((16,)),
            dma((16,)), dma((16,)),
            dma((4,)), dma((4,)),
            dma((8,)), dma((8,)),
            side_sems(), side_sems(),
        ],
        compiler_params=pltpu.CompilerParams(
            collective_id=1, has_side_effects=True, vmem_limit_bytes=60 * 2**20),
        cost_estimate=pl.CostEstimate(flops=5 * 10**9, bytes_accessed=10**7, transcendentals=0),
        name="rotate",
    )(act, grd, qa, qg, eig_in, eig_out)


def score_kernel(
    x_mine, y_mine, ids, corr, scores,
    x_all, y_all, id_all, rot, sq, sq_got, c_stage, acc, gram, red, red_got, red2, red2_got, blks,
    loc, gx_s, gx_r, gy_s, gy_r, id_s, id_r, sq_s, sq_r, t_s, t_r, o_s, o_r, f_s, f_r, p_s, p_r,
):
    h, c, y, x, z = place()
    oh, oc, oy = 1 - h, 1 - c, 1 - y
    yy = 2 * h + y
    xs = [lax.rem(x + d, 4) for d in range(4)]
    xb = [lax.rem(x + 4 - d, 4) for d in range(4)]
    zs = [lax.rem(z + d, 4) for d in range(4)]
    ys = [lax.rem(yy + d, 4) for d in range(4)]
    sibling = device(h, oc, y, x, z)
    greet(
        [sibling, device(h, c, oy, x, z), device(oh, c, oy, x, z)]
        + [device(h, c, y, xs[d], z) for d in (1, 2, 3)]
        + [device(oh, c, y, x, z)]
        + [device(h, c, y, x, zs[d]) for d in (1, 2, 3)]
    )
    started = []

    def go(copy):
        copy.start()
        started.append(copy)
        return copy

    groups = (pl.ds(0, 4), pl.ds(4, 5))

    def x_slot(t, xv, hv):
        return x_all[t].at[:, pl.ds(pl.multiple_of(128 * (2 * xv + hv), 128), 128), :]

    def y_slot(t, zv, yv):
        return y_all[t].at[:, :, pl.ds(pl.multiple_of(128 * (2 * zv + yv), 128), 128)]

    across_h, across_y = device(oh, c, y, x, z), device(h, c, oy, x, z)
    ids_copy = go(remote(ids, id_all.at[h], (id_s, id_r), 0, across_h))
    firsts, got = [], ([], [])
    for t in range(2):
        x_part, y_part = x_mine.at[groups[t]], y_mine.at[groups[t]]
        firsts.append((
            go(remote(x_part, x_slot(t, x, h), (gx_s, gx_r), 8 * t, across_h)),
            go(remote(y_part, y_slot(t, z, y), (gy_s, gy_r), 8 * t, across_y)),
        ))
    for t in range(2):
        x_part, y_part = x_mine.at[groups[t]], y_mine.at[groups[t]]
        for d in (1, 3, 2):
            got[t].append(go(remote(x_part, x_slot(t, x, h), (gx_s, gx_r), 8 * t + d, device(h, c, y, xs[d], z))))
            got[t].append(go(remote(y_part, y_slot(t, z, y), (gy_s, gy_r), 8 * t + d, device(h, c, y, x, zs[d]))))
        for copy in firsts[t]:
            copy.wait_recv()
        for d in (1, 3, 2):
            got[t].append(go(remote(
                x_slot(t, x, oh), x_slot(t, x, oh), (gx_s, gx_r), 8 * t + 4 + d, device(h, c, y, xs[d], z))))
            got[t].append(go(remote(
                y_slot(t, z, oy), y_slot(t, z, oy), (gy_s, gy_r), 8 * t + 4 + d, device(h, c, y, x, zs[d]))))
    local = [pltpu.make_async_copy(ids, id_all.at[h], loc.at[2])]
    for t in range(2):
        local.append(pltpu.make_async_copy(x_mine.at[groups[t]], x_slot(t, x, h), loc.at[4 * t]))
        local.append(pltpu.make_async_copy(y_mine.at[groups[t]], y_slot(t, z, y), loc.at[1 + 4 * t]))
    for copy in local:
        copy.start()
    sq[...] = jnp.zeros_like(sq)
    acc[...] = jnp.zeros_like(acc)
    for copy in local:
        copy.wait()
    ids_copy.wait_recv()
    for g in range(2):
        row = id_all[g]
        for e in range(EX):
            first = jnp.sum((row < e).astype(jnp.int32))
            blks[8 * g + e] = jnp.minimum(first // 128, 2)

    def quarter(kt, group):
        rows = pl.ds(pl.multiple_of(256 * kt, 256), 256)

        def pairs(m, _):
            lefts, blocks = [], []
            for u in range(4):
                n = 4 * m + u
                e = n - 8 * group
                blk = blks[n]
                parts = []
                for b in range(2):
                    keep = id_all[group, blk + b] == e
                    parts.append(jnp.where(keep, x_all[group][blk + b, rows, :].astype(F32), 0.0).astype(BF16))
                lefts.append(jnp.concatenate(parts, axis=1))
                blocks.append(blk)
            for it in range(4):
                cols = pl.ds(256 * it, 256)
                total = sq[kt, :, cols]
                for u in range(4):
                    right = jnp.concatenate([y_all[group][blocks[u], :, cols], y_all[group][blocks[u] + 1, :, cols]], axis=0)
                    value = jnp.dot(lefts[u], right, preferred_element_type=F32).astype(BF16)
                    rot[4 * m + u, rows, cols] = value
                    wide = value.astype(F32)
                    total = total + wide * wide
                sq[kt, :, cols] = total
            return 0

        lax.fori_loop(2 * group, 2 * group + 2, pairs, 0)

    def sq_copy(kt):
        return remote(sq.at[kt], sq_got.at[kt], (sq_s, sq_r), kt, sibling)

    def add_up(kt):
        sq_copy(kt).wait()

        def chunk(i, _):
            part = pl.ds(pl.multiple_of(32 * i, 32), 32)
            sq[kt, part, :] = (sq[kt, part, :] + sq_got[kt, part, :]) * (1.0 / 32.0)
            return 0

        lax.fori_loop(0, 8, chunk, 0)
        c_stage[kt] = sq[kt, pl.ds(pl.multiple_of(128 * c, 128), 128), :].astype(BF16)

    def norms(g, total):
        wide_ids = [jnp.broadcast_to(id_all[g, b].astype(F32), (128, 128)) for b in range(4)]
        tall_ids = [wide.T for wide in wide_ids]
        for a in range(4):
            for b in range(4):
                part = pl.ds(128 * b, 128)
                if abs(a - b) > 1:
                    gram[0, pl.ds(128 * a, 128), part] = jnp.zeros((128, 128), BF16)
                    gram[1, pl.ds(128 * a, 128), part] = jnp.zeros((128, 128), BF16)
                    continue
                value = lax.dot_general(
                    y_all[g][a], y_all[g][b], (((1,), (1,)), ((), ())), preferred_element_type=F32)
                value = jnp.where(tall_ids[a] == wide_ids[b], value, 0.0)
                high = value.astype(BF16)
                gram[0, pl.ds(128 * a, 128), part] = high
                gram[1, pl.ds(128 * a, 128), part] = (value - high.astype(F32)).astype(BF16)

        def chunk(i, total):
            rows = pl.ds(pl.multiple_of(256 * i, 256), 256)
            left = jnp.concatenate([x_all[g][b, rows, :] for b in range(4)], axis=1)
            value = jnp.dot(left, gram[0], preferred_element_type=F32)
            value += jnp.dot(left, gram[1], preferred_element_type=F32)
            value = value * left.astype(F32)
            for b in range(4):
                total = total + jnp.sum(value[:, 128 * b:128 * b + 128].reshape(32, 8, 128), axis=0)
            return total

        return lax.fori_loop(0, 4, chunk, total)

    def slab(xv, hv):
        return corr.at[2 * xv + hv, pl.ds(pl.multiple_of(128 * c, 128), 128), :]

    def out_copy(j):
        return remote(c_stage.at[xs[j]], slab(x, h), (o_s, o_r), j, device(h, c, y, xs[j], z))

    def cross(j):
        src = slab(xb[j], h) if j else c_stage.at[x]
        return remote(src, slab(xb[j], h), (o_s, o_r), 4 + j, across_h)

    own_out = pltpu.make_async_copy(c_stage.at[x], slab(x, h), loc.at[3])
    def at_y(v):
        return device(v // 2, c, lax.rem(v, 2), x, z)

    def over_x(d):
        return device(h, c, y, xs[d], z)

    def over_y(d):
        return at_y(ys[d])

    def over_z(d):
        return device(h, c, y, x, zs[d])

    def over_cores(d):
        return sibling

    class Spread:
        def __init__(self, value, axes, buf, got_buf, sems):
            self.value, self.axes, self.buf, self.got, self.sems, self.n = value, list(axes), buf, got_buf, sems, 0

        def start(self):
            n, (where, count) = self.n, self.axes[self.n]
            self.buf[n] = self.value
            self.copies = [
                go(remote(self.buf.at[n], self.got.at[n, d], self.sems, 3 * n + d, where(d + 1)))
                for d in range(count)]

        def wait(self):
            self.value = self.buf[self.n]
            for d, copy in enumerate(self.copies):
                copy.wait_recv()
                self.value = self.value + self.got[self.n, d]
            self.n += 1

    for copy in got[0]:
        copy.wait_recv()
    total = norms(0, jnp.zeros((8, 128), F32))
    for j in range(4):
        quarter(xs[j], 0)
    for copy in got[1]:
        copy.wait_recv()
    total = norms(1, total)
    whole = Spread(total, ((over_cores, 1), (over_x, 3), (over_y, 3), (over_z, 3)), red, red_got, (t_s, t_r))
    for j in range(4):
        whole.start()
        quarter(xs[j], 1)
        sq_copy(xs[j]).start()
        whole.wait()
        if j:
            add_up(xs[j - 1])
            if j == 1:
                cross(0).start()
                own_out.start()
            else:
                out_copy(j - 1).start()
    add_up(xs[3])
    out_copy(3).start()
    damping = 0.5 * (jnp.sum(whole.value) * (1.0 / 32.0) / (float(D_IN) * float(D_OUT)))

    def second(kt):
        rows = pl.ds(pl.multiple_of(256 * kt, 256), 256)

        def invert(i, _):
            part = pl.ds(pl.multiple_of(32 * i, 32), 32)
            sq[kt, part, :] = 1.0 / (sq[kt, part, :] + damping)
            return 0

        lax.fori_loop(0, 8, invert, 0)

        def pairs(m, _):
            query_in = x_all[1][4, rows, :].astype(F32)
            sums = [None] * 4
            for it in range(4):
                cols = pl.ds(256 * it, 256)
                factor = sq[kt, :, cols]
                query_out = y_all[1][4, :, cols]
                for u in range(4):
                    cond = (rot[4 * m + u, rows, cols].astype(F32) * factor).astype(BF16)
                    part = lax.dot_general(
                        cond, query_out, (((1,), (1,)), ((), ())), preferred_element_type=F32)
                    sums[u] = part if it == 0 else sums[u] + part
            for u in range(4):
                acc[pl.ds(4 * m + u, 1), :] += jnp.sum(sums[u] * query_in, axis=0, keepdims=True)
            return 0

        lax.fori_loop(0, EX // 2, pairs, 0)

    def hand_on(xv, hv):
        return remote(slab(xv, hv), slab(xv, hv), (f_s, f_r), 2 * xv + hv, sibling)

    def pass_on(j):
        if j:
            out_copy(j).wait()
            cross(j).start()
        else:
            own_out.wait()
        hand_on(xb[j], h).start()

    def take(j):
        cross(j).wait()
        hand_on(xb[j], oh).start()

    pass_on(1)
    second(xs[0])
    pass_on(2)
    second(xs[1])
    pass_on(3)
    second(xs[2])
    pass_on(0)
    second(xs[3])
    result = Spread(acc[...], ((over_z, 3), (over_x, 3), (over_y, 3)), red2, red2_got, (p_s, p_r))
    result.start()
    take(0)
    result.wait()
    result.start()
    take(1)
    result.wait()
    result.start()
    take(2)
    result.wait()
    take(3)
    scores[...] = result.value
    for j in range(4):
        for hv in (h, oh):
            hand_on(xb[j], hv).wait()
    for copy in started:
        copy.wait_send()


def score(x_mine, y_mine, ids):
    dma = pltpu.SemaphoreType.DMA
    vmem = pl.BlockSpec(memory_space=pltpu.VMEM)
    return pl.pallas_call(
        score_kernel,
        out_shape=(jax.ShapeDtypeStruct((8, 256, 1024), BF16), jax.ShapeDtypeStruct((2 * EX, 128), F32)),
        in_specs=[vmem] * 3,
        out_specs=(pl.BlockSpec(memory_space=pltpu.VMEM), vmem),
        scratch_shapes=[
            (pltpu.VMEM((4, 1024, 128), BF16), pltpu.VMEM((5, 1024, 128), BF16)),
            (pltpu.VMEM((4, 128, 1024), BF16), pltpu.VMEM((5, 128, 1024), BF16)),
            pltpu.VMEM((2, 4, 1, 128), jnp.int32),
            pltpu.VMEM((2 * EX, 1024, 1024), BF16),
            pltpu.VMEM((4, 256, 1024), F32),
            pltpu.VMEM((4, 256, 1024), F32),
            pltpu.VMEM((4, 128, 1024), BF16),
            pltpu.VMEM((2 * EX, 128), F32),
            pltpu.VMEM((2, 512, 512), BF16),
            pltpu.VMEM((4, 8, 128), F32),
            pltpu.VMEM((4, 3, 8, 128), F32),
            pltpu.VMEM((3, 2 * EX, 128), F32),
            pltpu.VMEM((3, 3, 2 * EX, 128), F32),
            pltpu.SMEM((2 * EX,), jnp.int32),
            dma((6,)),
            dma((16,)), dma((16,)),
            dma((16,)), dma((16,)),
            dma((1,)), dma((1,)),
            dma((4,)), dma((4,)),
            dma((12,)), dma((12,)),
            dma((8,)), dma((8,)),
            dma((8,)), dma((8,)),
            dma((9,)), dma((9,)),
        ],
        compiler_params=pltpu.CompilerParams(
            collective_id=2, has_side_effects=True, vmem_limit_bytes=60 * 2**20),
        cost_estimate=pl.CostEstimate(flops=2 * 10**10, bytes_accessed=10**7, transcendentals=0),
        name="score",
    )(x_mine, y_mine, ids)


def widen_kernel(corr, sums, out, scores, got, stage, got_sems, sems):
    def fetch(xv):
        return pltpu.make_async_copy(corr.at[pl.ds(2 * xv, 2)], got.at[pl.ds(2 * xv, 2)], got_sems.at[xv])

    def copy(n):
        xv, yv = n // 2, n % 2
        return pltpu.make_async_copy(stage.at[n % 4], out.at[:, pl.ds(1024 * (4 * yv + xv), 1024)], sems.at[n % 4])

    for xv in range(4):
        fetch(xv).start()
    for n in range(8):
        xv, yv = n // 2, n % 2
        if yv == 0:
            fetch(xv).wait()
        if n >= 4:
            copy(n - 4).wait()
        for zv in range(4):
            for hv in range(2):
                stage[n % 4, :, pl.ds(128 * (2 * zv + hv), 128)] = got[
                    2 * xv + hv, :, pl.ds(128 * (2 * zv + yv), 128)].astype(F32)
        copy(n).start()
    h = lax.axis_index("dp") // 2
    token = lax.broadcasted_iota(jnp.int32, (NQ * QTOK, NQ), 0)
    query = lax.broadcasted_iota(jnp.int32, (NQ * QTOK, NQ), 1)
    member = (token // QTOK == query).astype(F32)
    scores[...] = jnp.dot(
        sums[pl.ds(pl.multiple_of(EX * h, EX), EX), :], member,
        preferred_element_type=F32, precision=lax.Precision.HIGHEST) * (float(D_IN) * float(D_OUT)) ** -0.5
    for n in range(4, 8):
        copy(n).wait()


def widen(corr, sums):
    return pl.pallas_call(
        widen_kernel,
        out_shape=(jax.ShapeDtypeStruct((256, D_OUT), F32), jax.ShapeDtypeStruct((EX, NQ), F32)),
        in_specs=[pl.BlockSpec(memory_space=pl.ANY), pl.BlockSpec(memory_space=pltpu.VMEM)],
        out_specs=(pl.BlockSpec(memory_space=pl.ANY), pl.BlockSpec(memory_space=pltpu.VMEM)),
        scratch_shapes=[
            pltpu.VMEM((8, 256, 1024), BF16), pltpu.VMEM((4, 256, 1024), F32),
            pltpu.SemaphoreType.DMA((4,)), pltpu.SemaphoreType.DMA((4,)),
        ],
        compiler_params=pltpu.CompilerParams(vmem_limit_bytes=60 * 2**20),
        name="widen",
    )(corr, sums)


def per_device(activations, out_grads, query_acts, query_grads, eig_in, eig_out, example_ids):
    x_mine, y_mine = rotate(activations, out_grads, query_acts, query_grads, eig_in, eig_out)
    corr, sums = score(x_mine, y_mine, example_ids.reshape(4, 1, 128))
    corrections, scores = widen(corr, sums)
    return corrections, scores.T


def solution(mesh):
    return jax.shard_map(
        per_device,
        mesh=mesh,
        in_specs=(
            P("dp", "fsdp"),
            P("dp", "fsdp"),
            P(None, "fsdp"),
            P(None, "fsdp"),
            P("fsdp", None),
            P("fsdp", None),
            P("dp", None),
        ),
        out_specs=(P("fsdp", None), P(None, "dp")),
        check_vma=False,
    )
```
